512 devices in a mesh: grp: 8 (over z_lo, core), blk: 64 (over y, x, z_hi).
Axes of the slice: x: 4, y: 8, z: 8 (z_hi: 2, z_lo: 4; z = z_hi * 4 + z_lo), core: 2. Of those that a mesh axis runs over, the one named last changes fastest.
Arguments:
- images: bfloat16 [196608, 1152], P(('grp', 'blk')), may hold values from -1 to 1
- texts: bfloat16 [196608, 1152], P(('grp', 'blk')), may hold values from -1 to 1
- row_pair_labels: int32 [196608], P(('grp', 'blk')), may hold values from 0 to 1535
- logit_scale_log: float32 [1], replicated, may hold values from -0.7 to 0.7
- logit_bias: float32 [1], replicated, may hold values from -3 to 0
Outputs:
- row_loss: float32 [196608], P(('grp', 'blk'))
- image_embed_gradient: bfloat16 [196608, 1152], P(('grp', 'blk'))
- text_embed_gradient: bfloat16 [196608, 1152], P(('grp', 'blk'))
The draws below stay inside these ranges and needn't reach their ends.
All inputs are finite; a program needn't handle non-finite values.
Results may differ from the reference program's by a relative error of at most 0.0049.
Values may be sent and summed in bfloat16 or wider, within the bound.
A program may use at most 64 MiB of HBM per device.

```python
import jax
import jax.numpy as jnp
from jax import lax

EMBED_WIDTH = 1152
BLOCK_PAIR_ROWS = 384
PAIRS = 196608
N_GRP = 8
N_BLK = 64


def set_ends(result, key, smallest, high):
    longest = result.shape.index(max(result.shape))
    spots = []
    for shift in (0, 1):
        where = [jax.random.randint(jax.random.fold_in(key, axis), (), 0, length) for axis, length in enumerate(result.shape)]
        where[longest] = (where[longest] + shift) % result.shape[longest]
        spots.append(tuple(where))
    return result.at[spots[0]].set(smallest).at[spots[1]].set(high)


def steps_of(stream_key, extent, cuts, smallest, top_value):
    level, own = 1.0, jax.random.fold_in(stream_key, 6)
    for dim, shards_of in cuts:
        steps = jnp.exp(jax.random.uniform(jax.random.fold_in(own, dim), (shards_of,), jnp.float32, smallest / len(cuts), top_value / len(cuts)))
        level = level * jnp.repeat(steps, extent[dim] // shards_of).reshape([-1 if axis == dim else 1 for axis in range(len(extent))])
    return level


def gaussian(rng, extent, spread, bound, cuts=(), kind=jnp.bfloat16):
    factor_of = steps_of(rng, extent, cuts, -0.22, 0.18) if cuts else 1.0
    values = jax.random.normal(rng, extent, jnp.float32) * spread * factor_of
    return jnp.minimum(jnp.maximum(values, -bound), bound).astype(kind)


def setup_inputs(seed: int = 0) -> dict:
    seeds = jax.random.split(jax.random.key(seed), 6)
    return {
        "images": gaussian(seeds[0], (PAIRS, EMBED_WIDTH), 0.17, 1.0, ((0, 512),)),
        "texts": gaussian(seeds[1], (PAIRS, EMBED_WIDTH), 0.17, 1.0, ((0, 512),)),
        "row_pair_labels": set_ends(jax.random.randint(seeds[2], (PAIRS,), 0, 4 * BLOCK_PAIR_ROWS), jax.random.fold_in(seeds[2], 1), 0, (4 * BLOCK_PAIR_ROWS) - 1).astype(jnp.int32),
        "logit_scale_log": jnp.clip(jax.random.uniform(seeds[3], (1,), jnp.float32, -0.7, 0.7), -0.7, 0.7),
        "logit_bias": jnp.clip(jax.random.uniform(seeds[4], (1,), jnp.float32, -3.0, 0.0), -3.0, 0.0),
    }


def block_loss_terms(image_block_rows, image_pair_labels, text_block_rows, text_pair_labels, logit_multiplier, block_shift):
    pair_logits = logit_multiplier * lax.dot_general(image_block_rows, text_block_rows, (((1,), (1,)), ((), ())), preferred_element_type=jnp.float32) + block_shift
    positive_match = (image_pair_labels[:, None] == text_pair_labels[None, :]).astype(jnp.float32)
    row_sum = jnp.sum(jax.nn.softplus(pair_logits) - positive_match * pair_logits, axis=1)
    coefficient = (jax.nn.sigmoid(pair_logits) - positive_match).astype(jnp.bfloat16)
    image_part = jnp.dot(coefficient, text_block_rows, preferred_element_type=jnp.float32)
    text_part = lax.dot_general(coefficient, image_block_rows, (((0,), (0,)), ((), ())), preferred_element_type=jnp.float32)
    return row_sum, image_part, text_part


def reference(images, texts, row_pair_labels, logit_scale_log, logit_bias):
    logit_multiplier = jnp.exp(logit_scale_log[0])
    block_shift = logit_bias[0]
    text_block_list = N_GRP * N_BLK
    image_blocks = images.reshape(text_block_list, BLOCK_PAIR_ROWS, EMBED_WIDTH)
    image_pair_labels = row_pair_labels.reshape(text_block_list, BLOCK_PAIR_ROWS)
    text_grid = texts.reshape(N_GRP, N_BLK, BLOCK_PAIR_ROWS, EMBED_WIDTH)
    id_grid = row_pair_labels.reshape(N_GRP, N_BLK, BLOCK_PAIR_ROWS)
    row_sum = jnp.zeros((text_block_list, BLOCK_PAIR_ROWS), jnp.float32)
    image_gradient_sum = jnp.zeros((text_block_list, BLOCK_PAIR_ROWS, EMBED_WIDTH), jnp.float32)
    text_gradient_sum = jnp.zeros((N_GRP, N_BLK, BLOCK_PAIR_ROWS, EMBED_WIDTH), jnp.float32)
    windows = ((0, 0), (0, 1), (0, 2), (1, 0))
    for hop_count, step_count in windows:
        visited = jnp.roll(jnp.roll(text_grid, step_count, axis=1), hop_count, axis=0).reshape(text_block_list, BLOCK_PAIR_ROWS, EMBED_WIDTH)
        visited_ids = jnp.roll(jnp.roll(id_grid, step_count, axis=1), hop_count, axis=0).reshape(text_block_list, BLOCK_PAIR_ROWS)

        def one_block(window_entries):
            return block_loss_terms(window_entries[0], window_entries[1], window_entries[2], window_entries[3], logit_multiplier, block_shift)

        loss_part, image_part, text_part = lax.map(one_block, (image_blocks, image_pair_labels, visited, visited_ids))
        row_sum = row_sum + loss_part
        image_gradient_sum = image_gradient_sum + image_part
        text_gradient_sum = text_gradient_sum + jnp.roll(jnp.roll(text_part.reshape(N_GRP, N_BLK, BLOCK_PAIR_ROWS, EMBED_WIDTH), -step_count, axis=1), -hop_count, axis=0)
    row_loss = (row_sum / (len(windows) * BLOCK_PAIR_ROWS)).reshape(text_block_list * BLOCK_PAIR_ROWS)
    image_embed_gradient = (logit_multiplier * image_gradient_sum).astype(jnp.bfloat16).reshape(text_block_list * BLOCK_PAIR_ROWS, EMBED_WIDTH)
    text_embed_gradient = (logit_multiplier * text_gradient_sum).astype(jnp.bfloat16).reshape(text_block_list * BLOCK_PAIR_ROWS, EMBED_WIDTH)
    return row_loss, image_embed_gradient, text_embed_gradient
```

```python
import functools
import jax
import jax.numpy as jnp
from jax import lax
from jax.experimental import pallas as pl
from jax.experimental.pallas import tpu as pltpu
from jax.sharding import PartitionSpec as P

MESH = pl.DeviceIdType.MESH
ROWS = 128


def kernel(
    groups, blocks, cfg,
    scale_ref, bias_ref, labels_ref, images_ref, texts_ref,
    loss_ref, image_out, text_out,
    held, labels, columns, total, losses,
    load_sem, send_sem, recv_sem, label_send, label_recv,
):
    g, k = lax.axis_index("grp"), lax.axis_index("blk")
    odd = lax.rem(g, 2)
    SR = cfg["send_rows"]
    chunks = held.shape[1] // ROWS
    pieces = held.shape[1] // SR
    lows = groups // 2
    deep = 2 * lows

    def at(dg, dk):
        return (lax.rem(g + dg + groups, groups), lax.rem(k + dk + blocks, blocks))

    def world(w, place):
        return (place[0] + w * (groups - 1 - 2 * place[0]), place[1] + w * (blocks - 1 - 2 * place[1]))

    def height(place):
        return lows * lax.rem(place[1], 2) + place[0] // 2

    def on_chip(z, core, place):
        z = lax.rem(z + 2 * deep, deep)
        return (2 * lax.rem(z, lows) + core, place[1] - lax.rem(place[1], 2) + z // lows)

    def inner(z):
        return jnp.where(lax.rem(z + 2 * deep, lows) < lows - 1, 1, 0)

    def way(place):
        return jnp.where(lax.rem(place[0], 2) == inner(place[0] // 2), 0, 1)

    def core_of(z, down):
        return inner(z) + down * (1 - 2 * inner(z))

    mine = world(odd, (g, k))
    z = height(mine)

    def passes_to(down):
        return world(odd, on_chip(z + 1 - 2 * down, 0, mine))

    def taken_from(down):
        source = z - 1 + 2 * down
        return world(odd, on_chip(source, core_of(source, down), mine))

    def ends_at(down):
        source = z - (lows - 1) * (1 - 2 * down)
        start = on_chip(source, core_of(source, down), mine)
        return world(odd, (start[0], lax.rem(start[1] + 1, blocks)))

    def first_to(w):
        place = world(w, (g, k))
        down = way(place)
        return world(w, on_chip(height(place) + 1 - 2 * down, 0, place)), down

    def last_from(w):
        place = world(w, (g, k))
        source = (place[0], lax.rem(place[1] + blocks - 1, blocks))
        down = way(source)
        return world(w, on_chip(height(source) + (lows - 1) * (1 - 2 * down), 0, source))

    targets = [at(0, 1), at(0, 2), at(1, 0), at(0, -1), at(0, -2), at(-1, 0)]
    text_first, text_down = first_to(0)
    image_first, image_down = first_to(1)
    peers = targets + [
        passes_to(0), passes_to(1), taken_from(0), taken_from(1), ends_at(0), ends_at(1),
        text_first, image_first, last_from(0), last_from(1),
    ]
    barrier = pltpu.get_barrier_semaphore()
    for peer in peers:
        pl.semaphore_signal(barrier, inc=1, device_id=peer, device_id_type=MESH)
    loads = [
        pltpu.make_async_copy(texts_ref, held.at[6], load_sem.at[0]),
        pltpu.make_async_copy(images_ref, held.at[7], load_sem.at[1]),
    ]
    for load in loads:
        load.start()
    labels[6, 0:chunks] = labels_ref[...]
    labels[7, 0:chunks] = labels_ref[...]
    pl.semaphore_wait(barrier, len(peers))

    def block_copy(source, slot, piece, flow, device):
        rows = pl.ds(pl.multiple_of(piece * SR, SR), SR)
        return pltpu.make_async_remote_copy(
            src_ref=source.at[rows], dst_ref=held.at[slot, rows],
            send_sem=send_sem.at[flow, piece], recv_sem=recv_sem.at[slot, piece],
            device_id=device, device_id_type=MESH,
        )

    def first(w, piece):
        if w == 0:
            return block_copy(texts_ref, 8 + 3 * text_down, piece, 0, text_first)
        return block_copy(images_ref, 8 + 3 * image_down, piece, 1, image_first)

    def along(w, piece):
        if w == 0:
            return block_copy(texts_ref, 1, piece, 2, targets[1])
        return block_copy(images_ref, 4, piece, 3, targets[4])

    partner = (g + 1 - 2 * odd, k)

    def beside(piece):
        return block_copy(held.at[6 + odd], 2 + 3 * odd, piece, 4, partner)

    def onward(down, hop, piece):
        buffer = 7 + 3 * down + hop
        end = ends_at(down)
        step_to = passes_to(down)
        final = hop == 3
        slot = jnp.where(final, 3 * odd, buffer + 1)
        device = (jnp.where(final, end[0], step_to[0]), jnp.where(final, end[1], step_to[1]))
        return block_copy(held.at[buffer], slot, piece, 4 + 3 * down + hop, device)

    label_copies = [
        pltpu.make_async_remote_copy(
            src_ref=labels.at[6], dst_ref=labels.at[slot],
            send_sem=label_send.at[slot], recv_sem=label_recv.at[slot],
            device_id=targets[slot], device_id_type=MESH,
        )
        for slot in range(6)
    ]

    for piece in range(pieces):
        first(0, piece).start()
        first(1, piece).start()
    for copy in label_copies:
        copy.start()
    for piece in range(pieces):
        along(0, piece).start()
        along(1, piece).start()
    for load in loads:
        load.wait()
    for piece in range(pieces):
        beside(piece).start()

    t = jnp.exp(jnp.full((1, ROWS), scale_ref[0], jnp.float32))
    b = bias_ref[0]
    for c in range(chunks):
        row = labels_ref[c : c + 1, :].astype(jnp.float32)
        columns[c * ROWS : (c + 1) * ROWS] = jnp.transpose(jnp.broadcast_to(row, (ROWS, ROWS)))
    total[...] = jnp.zeros_like(total)
    losses[...] = jnp.zeros_like(losses)

    def step(side, buffer, slot, chunk):
        rows = pl.ds(pl.multiple_of(chunk * ROWS, ROWS), ROWS)
        moving = held[buffer, rows]
        logit = t * lax.dot_general(
            held[7 - side], moving, (((1,), (1,)), ((), ())), preferred_element_type=jnp.float32
        ) + b
        match = columns[...] == labels[slot, pl.ds(chunk, 1)].astype(jnp.float32)
        small = jnp.exp(-jnp.abs(logit))
        loss = jnp.maximum(logit, 0.0) + jnp.log1p(small) - jnp.where(match, logit, 0.0)
        gate = jnp.where(logit >= 0.0, 1.0, small) / (1.0 + small)
        coefficient = (gate - jnp.where(match, 1.0, 0.0)).astype(jnp.bfloat16)
        losses[side] += loss
        total[side] += jnp.dot(coefficient, moving, preferred_element_type=jnp.float32)

    def arrive(slot, piece):
        rows = pl.ds(pl.multiple_of(piece * SR, SR), SR)
        pltpu.make_async_copy(held.at[slot, rows], held.at[slot, rows], recv_sem.at[slot, piece]).wait()

    def arrive_rows(slot, chunk):
        for q in range(ROWS // SR):
            arrive(slot, chunk * (ROWS // SR) + q)

    def pass_on(hop, chunk):
        for q in range(ROWS // SR):
            for down in range(2):
                piece = chunk * (ROWS // SR) + q
                arrive(7 + 3 * down + hop, piece)
                onward(down, hop, piece).start()

    near = 5 - 3 * odd
    nearby = 8 + jnp.where(mine[0] == 0, 5, 0)

    def labels_arrive(slot):
        pltpu.make_async_copy(labels.at[slot], labels.at[slot], label_recv.at[slot]).wait()

    for slot in range(6):
        labels_arrive(slot)

    def rounds(n, carry):
        hop, chunk = n // chunks + 1, lax.rem(n, chunks)
        pass_on(hop, chunk)

        @pl.when(hop == 2)
        def _():
            arrive_rows(near, chunk)
            arrive_rows(1, chunk)

        @pl.when(hop == 3)
        def _():
            arrive_rows(4, chunk)

        if cfg["compute"]:
            buffer_a = jnp.where(hop == 1, 6, jnp.where(hop == 2, near, 4))
            side_a = jnp.where(hop == 1, 0, jnp.where(hop == 2, 1 - odd, 1))
            buffer_b = jnp.where(hop == 1, 7, jnp.where(hop == 2, 1, nearby))
            side_b = jnp.where(hop == 1, 1, jnp.where(hop == 2, 0, odd))
            slot_b = jnp.where(hop == 3, 2 + 3 * odd, buffer_b)

            def pair(i, carry):
                step(
                    jnp.where(i == 0, side_a, side_b), jnp.where(i == 0, buffer_a, buffer_b),
                    jnp.where(i == 0, buffer_a, slot_b), chunk,
                )
                return carry

            lax.fori_loop(0, 2, pair, 0)
        return carry

    lax.fori_loop(0, 3 * chunks, rounds, 0)

    def ends(n, carry):
        slot, chunk = 3 * lax.rem(n, 2), n // 2
        arrive_rows(slot, chunk)
        if cfg["compute"]:
            step(lax.rem(n, 2), slot, slot, chunk)
        return carry

    lax.fori_loop(0, 2 * chunks, ends, 0)

    for side, out in ((0, image_out), (1, text_out)):
        out[...] = (jnp.tile(t, (1, out.shape[1] // ROWS)) * total[side]).astype(jnp.bfloat16)
    for c in range(chunks):
        part = losses[0, c * ROWS : (c + 1) * ROWS]
        loss_ref[c : c + 1, :] = jnp.sum(jnp.transpose(part), axis=0, keepdims=True) * (
            1.0 / (4 * held.shape[1])
        )
    for copy in label_copies:
        copy.wait_send()
    for piece in range(pieces):
        first(0, piece).wait_send()
        first(1, piece).wait_send()
        along(0, piece).wait_send()
        along(1, piece).wait_send()
        beside(piece).wait_send()
        for down in range(2):
            for hop in (1, 2, 3):
                onward(down, hop, piece).wait_send()


def per_device(groups, blocks, cfg, images, texts, row_pair_labels, logit_scale_log, logit_bias):
    rows, width = images.shape
    chunks = rows // ROWS
    pieces = rows // cfg["send_rows"]
    vmem = pl.BlockSpec(memory_space=pltpu.VMEM)
    anywhere = pl.BlockSpec(memory_space=pl.ANY)
    smem = pl.BlockSpec(memory_space=pltpu.SMEM)
    loss, image_grad, text_grad = pl.pallas_call(
        functools.partial(kernel, groups, blocks, cfg),
        out_shape=(
            jax.ShapeDtypeStruct((chunks, ROWS), jnp.float32),
            jax.ShapeDtypeStruct((rows, width), jnp.bfloat16),
            jax.ShapeDtypeStruct((rows, width), jnp.bfloat16),
        ),
        in_specs=[smem, smem, vmem, anywhere, anywhere],
        out_specs=(vmem, vmem, vmem),
        scratch_shapes=[
            pltpu.VMEM((14, rows, width), jnp.bfloat16),
            pltpu.VMEM((8, 8, ROWS), jnp.int32),
            pltpu.VMEM((rows, ROWS), jnp.float32),
            pltpu.VMEM((2, rows, width), jnp.float32),
            pltpu.VMEM((2, rows, ROWS), jnp.float32),
            pltpu.SemaphoreType.DMA((2,)),
            pltpu.SemaphoreType.DMA((11, pieces)),
            pltpu.SemaphoreType.DMA((14, pieces)),
            pltpu.SemaphoreType.DMA((6,)),
            pltpu.SemaphoreType.DMA((6,)),
        ],
        compiler_params=pltpu.CompilerParams(
            collective_id=cfg.get("id", 0), has_side_effects=True, vmem_limit_bytes=60 << 20
        ),
        cost_estimate=pl.CostEstimate(
            flops=32 * rows * rows * width, bytes_accessed=8 * rows * width, transcendentals=24 * rows * rows
        ),
        name=cfg.get("name"),
    )(logit_scale_log, logit_bias, row_pair_labels.reshape(chunks, ROWS), images, texts)
    return loss.reshape(rows), image_grad, text_grad

CFG = {"compute": True, "send_rows": 128}

def solution(mesh):
    groups, blocks = mesh.shape["grp"], mesh.shape["blk"]
    both = P(("grp", "blk"))
    wide = P(("grp", "blk"), None)
    return jax.shard_map(
        functools.partial(per_device, groups, blocks, CFG),
        mesh=mesh,
        in_specs=(wide, wide, both, P(), P()),
        out_specs=(both, wide, wide),
        check_vma=False,
    )
```

```python
import functools
import jax
import jax.numpy as jnp
from jax import lax
from jax.experimental import pallas as pl
from jax.experimental.pallas import tpu as pltpu
from jax.sharding import PartitionSpec as P

MESH = pl.DeviceIdType.MESH
ROWS = 128
SEND = 128


def kernel(
    groups, blocks,
    scale_in, bias_in, labels_in, images_ref, texts_ref,
    loss_ref, image_out, text_out,
    held, labels, columns, total, losses, scale_ref, bias_ref,
    load_sem, send_sem, recv_sem, label_send, label_recv, ready,
):
    g, k = lax.axis_index("grp"), lax.axis_index("blk")
    odd = lax.rem(g, 2)
    chunks = held.shape[1] // ROWS
    pieces = held.shape[1] // SEND
    lows = groups // 2
    deep = 2 * lows

    def at(dg, dk):
        return (lax.rem(g + dg + groups, groups), lax.rem(k + dk + blocks, blocks))

    def world(w, place):
        return (place[0] + w * (groups - 1 - 2 * place[0]), place[1] + w * (blocks - 1 - 2 * place[1]))

    def height(place):
        return lows * lax.rem(place[1], 2) + place[0] // 2

    def on_chip(z, core, place):
        z = lax.rem(z + 2 * deep, deep)
        return (2 * lax.rem(z, lows) + core, place[1] - lax.rem(place[1], 2) + z // lows)

    def inner(z):
        return jnp.where(lax.rem(z + 2 * deep, lows) < lows - 1, 1, 0)

    def way(place):
        return jnp.where(lax.rem(place[0], 2) == inner(place[0] // 2), 0, 1)

    def core_of(z, down):
        return inner(z) + down * (1 - 2 * inner(z))

    mine = world(odd, (g, k))
    z = height(mine)

    def moved(place, yes):
        return (place[0], lax.rem(place[1] + 2 * yes + blocks, blocks))

    def turns(down, hop, source):
        source = lax.rem(source + 2 * deep, deep)
        if down == 0:
            return jnp.where(hop == 1, source // lows, 0)
        return jnp.where(hop == 3 - inner(source), source // lows, 0)

    def goes_to(down, hop):
        up = 1 - 2 * down
        source = z - hop * up
        core = jnp.where(hop == 3, core_of(source, down), 0)
        return world(odd, moved(on_chip(z + up, core, mine), turns(down, hop, source)))

    def first_to(w):
        place = world(w, (g, k))
        down = way(place)
        return world(w, on_chip(height(place) + 1 - 2 * down, 0, place)), down

    targets = [at(0, 1), at(0, 2), at(1, 0), at(0, -1), at(0, -2), at(-1, 0)]
    text_first, text_down = first_to(0)
    image_first, image_down = first_to(1)
    z_here = height((g, k))
    low = g // 2
    near_z = [on_chip(z_here + 1, 0, (g, k)), on_chip(z_here - 1, 0, (g, k))]
    far = [
        moved(on_chip(z_here + up, 1, (g, k)), side) for side in (-1, 1) for up in (-1, 0, 1)
    ] + [(2 * low + 1, at(0, 1)[1]), (2 * low + 1, at(0, -1)[1]), (2 * (lows - 1 - low) + 1, k)]
    partner = (g + 1 - 2 * odd, k)
    loads = [
        pltpu.make_async_copy(labels_in, labels.at[6], load_sem.at[2]),
        pltpu.make_async_copy(texts_ref, held.at[6], load_sem.at[0]),
        pltpu.make_async_copy(images_ref, held.at[7], load_sem.at[1]),
        pltpu.make_async_copy(scale_in, scale_ref, load_sem.at[3]),
        pltpu.make_async_copy(bias_in, bias_ref, load_sem.at[4]),
        pltpu.make_async_copy(labels_in, labels.at[7], load_sem.at[5]),
    ]
    barrier = pltpu.get_barrier_semaphore()
    for peer in near_z + [partner] + far:
        pl.semaphore_signal(barrier, inc=1, device_id=peer, device_id_type=MESH)
    for load in loads:
        load.start()

    @pl.when(odd == 0)
    def _():
        pl.semaphore_wait(barrier, 2 * len(near_z) + 1)
        pl.semaphore_signal(ready, inc=1, device_id=partner, device_id_type=MESH)

    @pl.when(odd == 1)
    def _():
        pl.semaphore_wait(ready, 1)

    def block_copy(source, slot, piece, flow, device):
        rows = pl.ds(pl.multiple_of(piece * SEND, SEND), SEND)
        return pltpu.make_async_remote_copy(
            src_ref=source.at[rows], dst_ref=held.at[slot, rows],
            send_sem=send_sem.at[flow, piece], recv_sem=recv_sem.at[slot, piece],
            device_id=device, device_id_type=MESH,
        )

    def first(w, piece):
        if w == 0:
            return block_copy(texts_ref, 8 + 3 * text_down, piece, 0, text_first)
        return block_copy(images_ref, 8 + 3 * image_down, piece, 1, image_first)

    def along(w, piece):
        if w == 0:
            return block_copy(texts_ref, 1, piece, 2, targets[1])
        return block_copy(images_ref, 4, piece, 3, targets[4])

    def beside(piece):
        return block_copy(held.at[6 + odd], 2 + 3 * odd, piece, 4, partner)

    def onward(down, hop, piece):
        buffer = 7 + 3 * down + hop
        slot = jnp.where(hop == 3, 3 * odd, buffer + 1)
        return block_copy(held.at[buffer], slot, piece, 4 + 3 * down + hop, goes_to(down, hop))

    label_copies = [
        pltpu.make_async_remote_copy(
            src_ref=labels_in, dst_ref=labels.at[slot],
            send_sem=label_send.at[slot], recv_sem=label_recv.at[slot],
            device_id=targets[slot], device_id_type=MESH,
        )
        for slot in range(6)
    ]

    for piece in range(pieces):
        first(0, piece).start()
        first(1, piece).start()

    @pl.when(odd == 1)
    def _():
        pl.semaphore_wait(barrier, 2 * len(far) + 1)
        pl.semaphore_signal(ready, inc=1, device_id=partner, device_id_type=MESH)

    @pl.when(odd == 0)
    def _():
        pl.semaphore_wait(ready, 1)

    for copy in label_copies:
        copy.start()
    for piece in range(pieces):
        along(0, piece).start()
        along(1, piece).start()
    for load in loads:
        load.wait()
    for piece in range(pieces):
        beside(piece).start()

    t = jnp.exp(jnp.full((1, ROWS), scale_ref[0], jnp.float32))
    b = bias_ref[0]
    for c in range(chunks):
        row = labels[6, c : c + 1, :].astype(jnp.float32)
        columns[c * ROWS : (c + 1) * ROWS] = jnp.transpose(jnp.broadcast_to(row, (ROWS, ROWS)))
    total[...] = jnp.zeros_like(total)
    losses[...] = jnp.zeros_like(losses)

    def step(side, buffer, slot, chunk):
        rows = pl.ds(pl.multiple_of(chunk * ROWS, ROWS), ROWS)
        moving = held[buffer, rows]
        logit = t * lax.dot_general(
            held[7 - side], moving, (((1,), (1,)), ((), ())), preferred_element_type=jnp.float32
        ) + b
        match = columns[...] == labels[slot, pl.ds(chunk, 1)].astype(jnp.float32)
        small = jnp.exp(-jnp.abs(logit))
        loss = jnp.maximum(logit, 0.0) + jnp.log1p(small) - jnp.where(match, logit, 0.0)
        gate = jnp.where(logit >= 0.0, 1.0, small) / (1.0 + small)
        coefficient = (gate - jnp.where(match, 1.0, 0.0)).astype(jnp.bfloat16)
        losses[side] += loss
        total[side] += jnp.dot(coefficient, moving, preferred_element_type=jnp.float32)

    def arrive(slot, piece):
        rows = pl.ds(pl.multiple_of(piece * SEND, SEND), SEND)
        pltpu.make_async_copy(held.at[slot, rows], held.at[slot, rows], recv_sem.at[slot, piece]).wait()

    def arrive_rows(slot, chunk):
        for q in range(ROWS // SEND):
            arrive(slot, chunk * (ROWS // SEND) + q)

    def pass_on(hop, chunk):
        for q in range(ROWS // SEND):
            for down in range(2):
                piece = chunk * (ROWS // SEND) + q
                arrive(7 + 3 * down + hop, piece)
                onward(down, hop, piece).start()

    near = 5 - 3 * odd
    nearby = 8 + jnp.where(mine[0] == 0, 5, 0)

    def labels_arrive(slot):
        pltpu.make_async_copy(labels.at[slot], labels.at[slot], label_recv.at[slot]).wait()

    def rounds(n, carry):
        hop, chunk = n // chunks + 1, lax.rem(n, chunks)
        pass_on(hop, chunk)

        @pl.when(n == chunks)
        def _():
            labels_arrive(near)
            labels_arrive(1)

        @pl.when(n == 2 * chunks)
        def _():
            labels_arrive(4)
            labels_arrive(2 + 3 * odd)

        @pl.when(hop == 2)
        def _():
            arrive_rows(near, chunk)
            arrive_rows(1, chunk)

        @pl.when(hop == 3)
        def _():
            arrive_rows(4, chunk)

        buffer_a = jnp.where(hop == 1, 6, jnp.where(hop == 2, near, 4))
        side_a = jnp.where(hop == 1, 0, jnp.where(hop == 2, 1 - odd, 1))
        buffer_b = jnp.where(hop == 1, 7, jnp.where(hop == 2, 1, nearby))
        side_b = jnp.where(hop == 1, 1, jnp.where(hop == 2, 0, odd))
        slot_b = jnp.where(hop == 3, 2 + 3 * odd, buffer_b)

        def pair(i, carry):
            step(
                jnp.where(i == 0, side_a, side_b), jnp.where(i == 0, buffer_a, buffer_b),
                jnp.where(i == 0, buffer_a, slot_b), chunk,
            )
            return carry

        lax.fori_loop(0, 2, pair, 0)
        return carry

    lax.fori_loop(0, 3 * chunks, rounds, 0)

    def finish(side, chunk):
        slot = 3 * side
        arrive_rows(slot, chunk)
        step(side, slot, slot, chunk)

    def ends(n, carry):
        finish(lax.rem(n, 2), n // 2)
        return carry

    labels_arrive(0)
    labels_arrive(3)
    lax.fori_loop(0, 2 * (chunks - 1), ends, 0)
    for side, out in ((0, image_out), (1, text_out)):
        finish(side, chunks - 1)
        out[...] = (jnp.tile(t, (1, out.shape[1] // ROWS)) * total[side]).astype(jnp.bfloat16)
    for c in range(chunks):
        part = losses[0, c * ROWS : (c + 1) * ROWS]
        loss_ref[c : c + 1, :] = jnp.sum(jnp.transpose(part), axis=0, keepdims=True) * (
            1.0 / (4 * held.shape[1])
        )
    for copy in label_copies:
        copy.wait_send()
    for piece in range(pieces):
        first(0, piece).wait_send()
        first(1, piece).wait_send()
        along(0, piece).wait_send()
        along(1, piece).wait_send()
        beside(piece).wait_send()
        for down in range(2):
            for hop in (1, 2, 3):
                onward(down, hop, piece).wait_send()


def per_device(groups, blocks, images, texts, row_pair_labels, logit_scale_log, logit_bias):
    rows, width = images.shape
    chunks = rows // ROWS
    pieces = rows // SEND
    vmem = pl.BlockSpec(memory_space=pltpu.VMEM)
    hbm = pl.BlockSpec(memory_space=pltpu.HBM)
    loss, image_grad, text_grad = pl.pallas_call(
        functools.partial(kernel, groups, blocks),
        out_shape=(
            jax.ShapeDtypeStruct((chunks, ROWS), jnp.float32),
            jax.ShapeDtypeStruct((rows, width), jnp.bfloat16),
            jax.ShapeDtypeStruct((rows, width), jnp.bfloat16),
        ),
        in_specs=[hbm] * 5,
        out_specs=(vmem, vmem, vmem),
        scratch_shapes=[
            pltpu.VMEM((14, rows, width), jnp.bfloat16),
            pltpu.VMEM((8, chunks, ROWS), jnp.int32),
            pltpu.VMEM((rows, ROWS), jnp.float32),
            pltpu.VMEM((2, rows, width), jnp.float32),
            pltpu.VMEM((2, rows, ROWS), jnp.float32),
            pltpu.SMEM((1,), jnp.float32),
            pltpu.SMEM((1,), jnp.float32),
            pltpu.SemaphoreType.DMA((6,)),
            pltpu.SemaphoreType.DMA((11, pieces)),
            pltpu.SemaphoreType.DMA((14, pieces)),
            pltpu.SemaphoreType.DMA((6,)),
            pltpu.SemaphoreType.DMA((6,)),
            pltpu.SemaphoreType.REGULAR,
        ],
        compiler_params=pltpu.CompilerParams(
            collective_id=0, has_side_effects=True, vmem_limit_bytes=52 << 20
        ),
        cost_estimate=pl.CostEstimate(
            flops=32 * rows * rows * width, bytes_accessed=8 * rows * width, transcendentals=24 * rows * rows
        ),
    )(
        logit_scale_log,
        logit_bias,
        *(
            pltpu.with_memory_space_constraint(a, pltpu.HBM)
            for a in (row_pair_labels.reshape(chunks, ROWS), images, texts)
        ),
    )
    return loss.reshape(rows), image_grad, text_grad


def solution(mesh):
    groups, blocks = mesh.shape["grp"], mesh.shape["blk"]
    both = P(("grp", "blk"))
    wide = P(("grp", "blk"), None)
    return jax.shard_map(
        functools.partial(per_device, groups, blocks),
        mesh=mesh,
        in_specs=(wide, wide, both, P(), P()),
        out_specs=(both, wide, wide),
        check_vma=False,
    )
```

```python
import functools
import jax
import jax.numpy as jnp
from jax import lax
from jax.experimental import pallas as pl
from jax.experimental.pallas import tpu as pltpu
from jax.sharding import PartitionSpec as P

MESH = pl.DeviceIdType.MESH
ROWS = 128
SEND = 128


def pairs(still, moving, still_labels, moving_labels, t, b):
    logit = t * lax.dot_general(
        still, moving, (((1,), (1,)), ((), ())), preferred_element_type=jnp.float32
    ) + b
    match = still_labels == moving_labels
    small = jnp.exp(-jnp.abs(logit))
    loss = jnp.maximum(logit, 0.0) + jnp.log1p(small) - jnp.where(match, logit, 0.0)
    gate = jnp.where(logit >= 0.0, 1.0, small) / (1.0 + small)
    return loss, (gate - jnp.where(match, 1.0, 0.0)).astype(jnp.bfloat16)


def kernel(
    groups, blocks,
    scale_ref, bias_ref, labels_in, images_ref, texts_ref,
    total, losses, columns, own, last, marks,
    held, labels,
    load_sem, send_sem, recv_sem, label_send, label_recv, ready,
):
    g, k = lax.axis_index("grp"), lax.axis_index("blk")
    odd = lax.rem(g, 2)
    chunks = held.shape[1] // ROWS
    pieces = held.shape[1] // SEND
    lows = groups // 2
    deep = 2 * lows

    def at(dg, dk):
        return (lax.rem(g + dg + groups, groups), lax.rem(k + dk + blocks, blocks))

    def world(w, place):
        return (place[0] + w * (groups - 1 - 2 * place[0]), place[1] + w * (blocks - 1 - 2 * place[1]))

    def height(place):
        return lows * lax.rem(place[1], 2) + place[0] // 2

    def on_chip(z, core, place):
        z = lax.rem(z + 2 * deep, deep)
        return (2 * lax.rem(z, lows) + core, place[1] - lax.rem(place[1], 2) + z // lows)

    def inner(z):
        return jnp.where(lax.rem(z + 2 * deep, lows) < lows - 1, 1, 0)

    def way(place):
        return jnp.where(lax.rem(place[0], 2) == inner(place[0] // 2), 0, 1)

    def core_of(z, down):
        return inner(z) + down * (1 - 2 * inner(z))

    mine = world(odd, (g, k))
    z = height(mine)

    def moved(place, yes):
        return (place[0], lax.rem(place[1] + 2 * yes + blocks, blocks))

    def turns(down, hop, source):
        source = lax.rem(source + 2 * deep, deep)
        if down == 0:
            return jnp.where(hop == 1, source // lows, 0)
        return jnp.where(hop == 3 - inner(source), source // lows, 0)

    def goes_to(down, hop):
        up = 1 - 2 * down
        source = z - hop * up
        core = jnp.where(hop == 3, core_of(source, down), 0)
        return world(odd, moved(on_chip(z + up, core, mine), turns(down, hop, source)))

    def first_to(w):
        place = world(w, (g, k))
        down = way(place)
        return world(w, on_chip(height(place) + 1 - 2 * down, 0, place)), down

    targets = [at(0, 1), at(0, 2), at(1, 0), at(0, -1), at(0, -2), at(-1, 0)]
    text_first, text_down = first_to(0)
    image_first, image_down = first_to(1)
    z_here = height((g, k))
    low = g // 2
    near_z = [on_chip(z_here + 1, 0, (g, k)), on_chip(z_here - 1, 0, (g, k))]
    far = [
        moved(on_chip(z_here + up, 1, (g, k)), side) for side in (-1, 1) for up in (-1, 0, 1)
    ] + [(2 * low + 1, at(0, 1)[1]), (2 * low + 1, at(0, -1)[1]), (2 * (lows - 1 - low) + 1, k)]
    partner = (g + 1 - 2 * odd, k)
    loads = [
        pltpu.make_async_copy(labels_in, labels.at[6], load_sem.at[2]),
        pltpu.make_async_copy(texts_ref, held.at[6], load_sem.at[0]),
        pltpu.make_async_copy(images_ref, held.at[7], load_sem.at[1]),
        pltpu.make_async_copy(labels_in, labels.at[7], load_sem.at[3]),
    ]
    barrier = pltpu.get_barrier_semaphore()
    for peer in near_z + [partner]:
        pl.semaphore_signal(barrier, inc=1, device_id=peer, device_id_type=MESH)

    @pl.when(odd == 0)
    def _():
        pl.semaphore_wait(barrier, 2 * len(near_z) + 1)
        pl.semaphore_signal(ready, inc=1, device_id=partner, device_id_type=MESH)

    @pl.when(odd == 1)
    def _():
        pl.semaphore_wait(ready, 1)

    def block_copy(source, slot, piece, flow, device):
        rows = pl.ds(pl.multiple_of(piece * SEND, SEND), SEND)
        return pltpu.make_async_remote_copy(
            src_ref=source.at[rows], dst_ref=held.at[slot, rows],
            send_sem=send_sem.at[flow, piece], recv_sem=recv_sem.at[slot, piece],
            device_id=device, device_id_type=MESH,
        )

    def first(w, piece):
        if w == 0:
            return block_copy(texts_ref, 8 + 3 * text_down, piece, 0, text_first)
        return block_copy(images_ref, 8 + 3 * image_down, piece, 1, image_first)

    def along(w, piece):
        if w == 0:
            return block_copy(texts_ref, 1, piece, 2, targets[1])
        return block_copy(images_ref, 4, piece, 3, targets[4])

    def beside(piece):
        return block_copy(held.at[6 + odd], 2 + 3 * odd, piece, 4, partner)

    def onward(down, hop, piece):
        buffer = 7 + 3 * down + hop
        slot = jnp.where(hop == 3, 3 * odd, buffer + 1)
        return block_copy(held.at[buffer], slot, piece, 4 + 3 * down + hop, goes_to(down, hop))

    label_copies = [
        pltpu.make_async_remote_copy(
            src_ref=labels_in, dst_ref=labels.at[slot],
            send_sem=label_send.at[slot], recv_sem=label_recv.at[slot],
            device_id=targets[slot], device_id_type=MESH,
        )
        for slot in range(6)
    ]

    for piece in range(pieces):
        first(0, piece).start()
        first(1, piece).start()
    for peer in far:
        pl.semaphore_signal(barrier, inc=1, device_id=peer, device_id_type=MESH)
    for load in loads:
        load.start()

    @pl.when(odd == 1)
    def _():
        pl.semaphore_wait(barrier, 2 * len(far) + 1)
        pl.semaphore_signal(ready, inc=1, device_id=partner, device_id_type=MESH)

    @pl.when(odd == 0)
    def _():
        pl.semaphore_wait(ready, 1)

    for copy in label_copies:
        copy.start()
    for piece in range(pieces):
        along(0, piece).start()
        along(1, piece).start()
    for load in loads:
        load.wait()
    for piece in range(pieces):
        beside(piece).start()

    t = jnp.exp(jnp.full((1, ROWS), scale_ref[0], jnp.float32))
    b = jnp.full((1, ROWS), bias_ref[0], jnp.float32)
    for c in range(chunks):
        row = labels[6, c : c + 1, :].astype(jnp.float32)
        columns[c * ROWS : (c + 1) * ROWS] = jnp.transpose(jnp.broadcast_to(row, (ROWS, ROWS)))
    total[...] = jnp.zeros_like(total)
    losses[...] = jnp.zeros_like(losses)

    marks[0:1] = t
    marks[1:2] = b
    for side in range(2):
        own[side] = held[7 - side]

    def step(side, buffer, slot, chunk):
        rows = pl.ds(pl.multiple_of(chunk * ROWS, ROWS), ROWS)
        moving = held[buffer, rows]
        loss, coefficient = pairs(
            held[7 - side], moving, columns[...], labels[slot, pl.ds(chunk, 1)].astype(jnp.float32), t, b
        )
        losses[side] += loss
        total[side] += jnp.dot(coefficient, moving, preferred_element_type=jnp.float32)

    def arrive(slot, piece):
        rows = pl.ds(pl.multiple_of(piece * SEND, SEND), SEND)
        pltpu.make_async_copy(held.at[slot, rows], held.at[slot, rows], recv_sem.at[slot, piece]).wait()

    def arrive_rows(slot, chunk):
        for q in range(ROWS // SEND):
            arrive(slot, chunk * (ROWS // SEND) + q)

    def pass_on(hop, chunk):
        for q in range(ROWS // SEND):
            for down in range(2):
                piece = chunk * (ROWS // SEND) + q
                arrive(7 + 3 * down + hop, piece)
                onward(down, hop, piece).start()

    near = 5 - 3 * odd
    nearby = 8 + jnp.where(mine[0] == 0, 5, 0)

    def labels_arrive(slot):
        pltpu.make_async_copy(labels.at[slot], labels.at[slot], label_recv.at[slot]).wait()

    def rounds(n, carry):
        hop, chunk = n // chunks + 1, lax.rem(n, chunks)
        pass_on(hop, chunk)

        @pl.when(n == chunks)
        def _():
            labels_arrive(near)
            labels_arrive(1)

        @pl.when(n == 2 * chunks)
        def _():
            labels_arrive(4)
            labels_arrive(2 + 3 * odd)

        @pl.when(hop == 2)
        def _():
            arrive_rows(near, chunk)
            arrive_rows(1, chunk)

        @pl.when(hop == 3)
        def _():
            arrive_rows(4, chunk)

        buffer_a = jnp.where(hop == 1, 6, jnp.where(hop == 2, near, 4))
        side_a = jnp.where(hop == 1, 0, jnp.where(hop == 2, 1 - odd, 1))
        buffer_b = jnp.where(hop == 1, 7, jnp.where(hop == 2, 1, nearby))
        side_b = jnp.where(hop == 1, 1, jnp.where(hop == 2, 0, odd))
        slot_b = jnp.where(hop == 3, 2 + 3 * odd, buffer_b)

        def pair(i, carry):
            step(
                jnp.where(i == 0, side_a, side_b), jnp.where(i == 0, buffer_a, buffer_b),
                jnp.where(i == 0, buffer_a, slot_b), chunk,
            )
            return carry

        lax.fori_loop(0, 2, pair, 0)
        return carry

    lax.fori_loop(0, 3 * chunks, rounds, 0)

    def finish(side, chunk):
        slot = 3 * side
        arrive_rows(slot, chunk)
        step(side, slot, slot, chunk)

    def ends(n, carry):
        finish(lax.rem(n, 2), n // 2)
        return carry

    labels_arrive(0)
    labels_arrive(3)
    lax.fori_loop(0, 2 * (chunks - 1), ends, 0)
    for side in range(2):
        arrive_rows(3 * side, chunks - 1)
        last[side] = held[3 * side, (chunks - 1) * ROWS :]
        marks[2 + side : 3 + side] = labels[3 * side, chunks - 1 :].astype(jnp.float32)
    for copy in label_copies:
        copy.wait_send()
    for piece in range(pieces):
        first(0, piece).wait_send()
        first(1, piece).wait_send()
        along(0, piece).wait_send()
        along(1, piece).wait_send()
        beside(piece).wait_send()
        for down in range(2):
            for hop in (1, 2, 3):
                onward(down, hop, piece).wait_send()


def finish_kernel(
    total, losses, columns, own, last, marks,
    loss_out, image_out, text_out,
    loss_ref, rounded, sems, loss_sem,
):
    chunks = own.shape[1] // ROWS
    t, b = marks[0:1], marks[1:2]
    wide_t = jnp.tile(t, (1, own.shape[2] // ROWS))
    copies = []
    both_sides = [
        pairs(own[side], last[side], columns[...], marks[2 + side : 3 + side], t, b) for side in range(2)
    ]
    for side, out in ((0, image_out), (1, text_out)):
        loss_all, coefficient_all = both_sides[side]
        for c in range(chunks):
            rows = pl.ds(c * ROWS, ROWS)
            loss = loss_all[c * ROWS : (c + 1) * ROWS]
            coefficient = coefficient_all[c * ROWS : (c + 1) * ROWS]
            grad = total[side, rows] + jnp.dot(coefficient, last[side], preferred_element_type=jnp.float32)
            rounded[side, rows] = (wide_t * grad).astype(jnp.bfloat16)
            copies.append(pltpu.make_async_copy(rounded.at[side, rows], out.at[rows], sems.at[side, c]))
            copies[-1].start()
            if side == 0:
                loss_ref[c : c + 1, :] = jnp.sum(
                    jnp.transpose(losses[0, rows] + loss), axis=0, keepdims=True
                ) * (1.0 / (4 * own.shape[1]))
        if side == 0:
            copies.append(pltpu.make_async_copy(loss_ref, loss_out, loss_sem))
            copies[-1].start()
    for copy in copies:
        copy.wait()


def per_device(groups, blocks, images, texts, row_pair_labels, logit_scale_log, logit_bias):
    rows, width = images.shape
    chunks = rows // ROWS
    pieces = rows // SEND
    vmem = pl.BlockSpec(memory_space=pltpu.VMEM)
    hbm = pl.BlockSpec(memory_space=pltpu.HBM)
    parts = pl.pallas_call(
        functools.partial(kernel, groups, blocks),
        out_shape=(
            pltpu.VMEM((2, rows, width), jnp.float32),
            pltpu.VMEM((2, rows, ROWS), jnp.float32),
            pltpu.VMEM((rows, ROWS), jnp.float32),
            pltpu.VMEM((2, rows, width), jnp.bfloat16),
            pltpu.VMEM((2, ROWS, width), jnp.bfloat16),
            pltpu.VMEM((8, ROWS), jnp.float32),
        ),
        in_specs=[pl.BlockSpec(memory_space=pltpu.SMEM)] * 2 + [hbm] * 3,
        out_specs=(vmem,) * 6,
        scratch_shapes=[
            pltpu.VMEM((14, rows, width), jnp.bfloat16),
            pltpu.VMEM((8, chunks, ROWS), jnp.int32),
            pltpu.SemaphoreType.DMA((4,)),
            pltpu.SemaphoreType.DMA((11, pieces)),
            pltpu.SemaphoreType.DMA((14, pieces)),
            pltpu.SemaphoreType.DMA((6,)),
            pltpu.SemaphoreType.DMA((6,)),
            pltpu.SemaphoreType.REGULAR,
        ],
        compiler_params=pltpu.CompilerParams(
            collective_id=0, has_side_effects=True, vmem_limit_bytes=40 << 20
        ),
        cost_estimate=pl.CostEstimate(
            flops=32 * rows * rows * width, bytes_accessed=8 * rows * width, transcendentals=24 * rows * rows
        ),
    )(
        logit_scale_log,
        logit_bias,
        *(
            pltpu.with_memory_space_constraint(a, pltpu.HBM)
            for a in (row_pair_labels.reshape(chunks, ROWS), images, texts)
        ),
    )
    loss, image_grad, text_grad = pl.pallas_call(
        finish_kernel,
        out_shape=(
            jax.ShapeDtypeStruct((chunks, ROWS), jnp.float32),
            jax.ShapeDtypeStruct((rows, width), jnp.bfloat16),
            jax.ShapeDtypeStruct((rows, width), jnp.bfloat16),
        ),
        in_specs=[vmem] * 6,
        out_specs=(hbm,) * 3,
        scratch_shapes=[
            pltpu.VMEM((chunks, ROWS), jnp.float32),
            pltpu.VMEM((2, rows, width), jnp.bfloat16),
            pltpu.SemaphoreType.DMA((2, chunks)),
            pltpu.SemaphoreType.DMA,
        ],
        compiler_params=pltpu.CompilerParams(vmem_limit_bytes=24 << 20),
    )(*(pltpu.with_memory_space_constraint(a, pltpu.VMEM) for a in parts))
    return loss.reshape(rows), image_grad, text_grad


def solution(mesh):
    groups, blocks = mesh.shape["grp"], mesh.shape["blk"]
    both = P(("grp", "blk"))
    wide = P(("grp", "blk"), None)
    return jax.shard_map(
        functools.partial(per_device, groups, blocks),
        mesh=mesh,
        in_specs=(wide, wide, both, P(), P()),
        out_specs=(both, wide, wide),
        check_vma=False,
    )
```

```python
import functools
import jax
import jax.numpy as jnp
from jax import lax
from jax.experimental import pallas as pl
from jax.experimental.pallas import tpu as pltpu
from jax.sharding import PartitionSpec as P

MESH = pl.DeviceIdType.MESH
ROWS = 128
SPLIT = 32


def pairs(still, moving, still_labels, moving_labels, t, b):
    logit = t * lax.dot_general(
        still, moving, (((1,), (1,)), ((), ())), preferred_element_type=jnp.float32
    ) + b
    match = still_labels == moving_labels
    small = jnp.exp(-jnp.abs(logit))
    loss = jnp.maximum(logit, 0.0) + jnp.log1p(small) - jnp.where(match, logit, 0.0)
    gate = jnp.where(logit >= 0.0, 1.0, small) / (1.0 + small)
    return loss, (gate - jnp.where(match, 1.0, 0.0)).astype(jnp.bfloat16)


def kernel(
    groups, blocks,
    scale_ref, bias_ref, labels_in, images_ref, texts_ref,
    total, losses, columns, own, last, marks,
    held, labels,
    load_sem, send_sem, recv_sem, label_send, label_recv, ready,
):
    g, k = lax.axis_index("grp"), lax.axis_index("blk")
    odd = lax.rem(g, 2)
    chunks = held.shape[1] // ROWS
    lows = groups // 2
    deep = 2 * lows

    def at(dg, dk):
        return (lax.rem(g + dg + groups, groups), lax.rem(k + dk + blocks, blocks))

    def world(w, place):
        return (place[0] + w * (groups - 1 - 2 * place[0]), place[1] + w * (blocks - 1 - 2 * place[1]))

    def height(place):
        return lows * lax.rem(place[1], 2) + place[0] // 2

    def on_chip(z, core, place):
        z = lax.rem(z + 2 * deep, deep)
        return (2 * lax.rem(z, lows) + core, place[1] - lax.rem(place[1], 2) + z // lows)

    z_here = height((g, k))
    near_z = [on_chip(z_here + 1, 0, (g, k)), on_chip(z_here - 1, 0, (g, k))]
    partner = (g + 1 - 2 * odd, k)
    barrier = pltpu.get_barrier_semaphore()
    for peer in near_z + [partner]:
        pl.semaphore_signal(barrier, inc=1, device_id=peer, device_id_type=MESH)
    block_loads = [
        [
            pltpu.make_async_copy(
                source.at[pl.ds(chunk * ROWS, ROWS)], held.at[slot, pl.ds(chunk * ROWS, ROWS)],
                load_sem.at[4 + 2 * chunk + slot - 6],
            )
            for source, slot in ((texts_ref, 6), (images_ref, 7))
        ]
        for chunk in range(chunks)
    ]
    for pair in block_loads:
        for load in pair:
            load.start()

    def inner(z):
        return jnp.where(lax.rem(z + 2 * deep, lows) < lows - 1, 1, 0)

    def way(place):
        return jnp.where(lax.rem(place[0], 2) == inner(place[0] // 2), 0, 1)

    def core_of(z, down):
        return inner(z) + down * (1 - 2 * inner(z))

    mine = world(odd, (g, k))
    z = height(mine)

    def moved(place, yes):
        return (place[0], lax.rem(place[1] + 2 * yes + blocks, blocks))

    def turns(down, hop, source):
        source = lax.rem(source + 2 * deep, deep)
        if down == 0:
            return jnp.where(hop == 1, source // lows, 0)
        return jnp.where(hop == 3 - inner(source), source // lows, 0)

    def goes_to(down, hop):
        up = 1 - 2 * down
        source = z - hop * up
        core = jnp.where(hop == 3, core_of(source, down), 0)
        return world(odd, moved(on_chip(z + up, core, mine), turns(down, hop, source)))

    def first_to(w):
        place = world(w, (g, k))
        down = way(place)
        return world(w, on_chip(height(place) + 1 - 2 * down, 0, place)), down

    targets = [at(0, 1), at(0, 2), at(1, 0), at(0, -1), at(0, -2), at(-1, 0)]
    text_first, text_down = first_to(0)
    image_first, image_down = first_to(1)
    low = g // 2
    far = [
        moved(on_chip(z_here + up, 1, (g, k)), side) for side in (-1, 1) for up in (-1, 0, 1)
    ] + [(2 * low + 1, at(0, 1)[1]), (2 * low + 1, at(0, -1)[1]), (2 * (lows - 1 - low) + 1, k)]
    loads = [
        pltpu.make_async_copy(labels_in, labels.at[6], load_sem.at[2]),
        pltpu.make_async_copy(labels_in, labels.at[7], load_sem.at[3]),
    ]
    @pl.when(odd == 0)
    def _():
        pl.semaphore_wait(barrier, 2 * len(near_z) + 1)
        pl.semaphore_signal(ready, inc=1, device_id=partner, device_id_type=MESH)

    @pl.when(odd == 1)
    def _():
        pl.semaphore_wait(ready, 1)

    tail = chunks * ROWS - SPLIT

    def rows_of(piece):
        if isinstance(piece, int) and piece >= chunks - 1:
            return pl.ds(tail, SPLIT) if piece == chunks else pl.ds((chunks - 1) * ROWS, ROWS - SPLIT)
        return pl.ds(pl.multiple_of(piece * ROWS, ROWS), ROWS)

    def block_copy(source, slot, piece, flow, device):
        rows = rows_of(piece)
        return pltpu.make_async_remote_copy(
            src_ref=source.at[rows], dst_ref=held.at[slot, rows],
            send_sem=send_sem.at[flow, piece], recv_sem=recv_sem.at[slot, piece],
            device_id=device, device_id_type=MESH,
        )

    def whole_copy(source, slot, chunk, flow, device):
        rows = pl.ds(chunk * ROWS, ROWS)
        return pltpu.make_async_remote_copy(
            src_ref=source.at[rows], dst_ref=held.at[slot, rows],
            send_sem=send_sem.at[flow, chunk], recv_sem=recv_sem.at[slot, chunk],
            device_id=device, device_id_type=MESH,
        )

    top = deep - 1
    down_to = world(
        odd,
        moved(
            on_chip(z + 2 * odd - 1, 0, mine), jnp.where(z_here == lows, 1 - odd, 0)
        ),
    )

    def first(w, piece):
        source, down, device = [(6, text_down, text_first), (7, image_down, image_first)][w]
        slot = 8 + 3 * down
        if piece == chunks:
            turned = jnp.where(odd == w, jnp.where(z_here == top, 1, 0), 0)
            slot = jnp.where(turned == 1, 14, slot)
            device = tuple(jnp.where(turned == 1, x, y) for x, y in zip(down_to, device))
        return block_copy(held.at[source], slot, piece, w, device)

    def short_down():
        slot = jnp.where(z_here == lows, 3 * odd, 14)
        return block_copy(held.at[14], slot, chunks, 11, down_to)

    def along(w, chunk):
        if w == 0:
            return whole_copy(held.at[6], 1, chunk, 2, targets[1])
        return whole_copy(held.at[7], 4, chunk, 3, targets[4])

    def beside(chunk):
        return whole_copy(held.at[6 + odd], 2 + 3 * odd, chunk, 4, partner)

    def onward(down, hop, piece):
        buffer = 7 + 3 * down + hop
        slot = jnp.where(hop == 3, 3 * odd, buffer + 1)
        return block_copy(held.at[buffer], slot, piece, 4 + 3 * down + hop, goes_to(down, hop))

    def is_short(down, hop):
        return jnp.where(odd == down, jnp.where(hop == z_here + 1, 1, 0), 0)

    label_copies = [
        pltpu.make_async_remote_copy(
            src_ref=labels_in, dst_ref=labels.at[slot],
            send_sem=label_send.at[slot], recv_sem=label_recv.at[slot],
            device_id=targets[slot], device_id_type=MESH,
        )
        for slot in range(6)
    ]

    for chunk in range(chunks):
        for load in block_loads[chunk]:
            load.wait()
        first(0, chunk).start()
        first(1, chunk).start()
    first(0, chunks).start()
    first(1, chunks).start()
    for peer in far:
        pl.semaphore_signal(barrier, inc=1, device_id=peer, device_id_type=MESH)
    for load in loads:
        load.start()

    @pl.when(odd == 1)
    def _():
        pl.semaphore_wait(barrier, 2 * len(far) + 1)
        pl.semaphore_signal(ready, inc=1, device_id=partner, device_id_type=MESH)

    @pl.when(odd == 0)
    def _():
        pl.semaphore_wait(ready, 1)

    for copy in label_copies:
        copy.start()
    for chunk in range(chunks):
        along(0, chunk).start()
        along(1, chunk).start()
    for load in loads:
        load.wait()
    for chunk in range(chunks):
        beside(chunk).start()

    t = jnp.exp(jnp.full((1, ROWS), scale_ref[0], jnp.float32))
    b = jnp.full((1, ROWS), bias_ref[0], jnp.float32)
    for c in range(chunks):
        row = labels[6, c : c + 1, :].astype(jnp.float32)
        columns[c * ROWS : (c + 1) * ROWS] = jnp.transpose(jnp.broadcast_to(row, (ROWS, ROWS)))
    total[...] = jnp.zeros_like(total)
    losses[...] = jnp.zeros_like(losses)

    marks[0:1] = t
    marks[1:2] = b
    for side in range(2):
        own[side] = held[7 - side]

    def step(side, buffer, slot, chunk):
        rows = pl.ds(pl.multiple_of(chunk * ROWS, ROWS), ROWS)
        moving = held[buffer, rows]
        loss, coefficient = pairs(
            held[7 - side], moving, columns[...], labels[slot, pl.ds(chunk, 1)].astype(jnp.float32), t, b
        )
        losses[side] += loss
        total[side] += jnp.dot(coefficient, moving, preferred_element_type=jnp.float32)

    def arrive(slot, piece):
        rows = rows_of(piece)
        pltpu.make_async_copy(held.at[slot, rows], held.at[slot, rows], recv_sem.at[slot, piece]).wait()

    def arrive_rows(slot, chunk):
        rows = pl.ds(pl.multiple_of(chunk * ROWS, ROWS), ROWS)
        pltpu.make_async_copy(held.at[slot, rows], held.at[slot, rows], recv_sem.at[slot, chunk]).wait()

    def pass_on(hop, chunk):
        for down in range(2):
            @pl.when(chunk < chunks - 1)
            def _():
                arrive(7 + 3 * down + hop, chunk)
                onward(down, hop, chunk).start()

            @pl.when(chunk == chunks - 1)
            def _():
                arrive(7 + 3 * down + hop, chunks - 1)
                onward(down, hop, chunks - 1).start()

                @pl.when(is_short(down, hop) == 0)
                def _():
                    arrive(7 + 3 * down + hop, chunks)
                    onward(down, hop, chunks).start()

    turned_at = jnp.where(
        z_here == top - 1, chunks, jnp.where(z_here == top - 2, 2 * chunks, jnp.where(z_here == lows, 3 * chunks - 1, -1))
    )

    near = 5 - 3 * odd
    nearby = 8 + jnp.where(mine[0] == 0, 5, 0)

    def labels_arrive(slot):
        pltpu.make_async_copy(labels.at[slot], labels.at[slot], label_recv.at[slot]).wait()

    def rounds(n, carry):
        hop, chunk = n // chunks + 1, lax.rem(n, chunks)
        pass_on(hop, chunk)

        @pl.when(n == turned_at)
        def _():
            arrive(14, chunks)
            short_down().start()

        @pl.when(n == chunks)
        def _():
            labels_arrive(near)
            labels_arrive(1)

        @pl.when(n == 2 * chunks)
        def _():
            labels_arrive(4)
            labels_arrive(2 + 3 * odd)

        @pl.when(hop == 2)
        def _():
            arrive_rows(near, chunk)
            arrive_rows(1, chunk)

        @pl.when(hop == 3)
        def _():
            arrive_rows(4, chunk)

        buffer_a = jnp.where(hop == 1, 6, jnp.where(hop == 2, near, 4))
        side_a = jnp.where(hop == 1, 0, jnp.where(hop == 2, 1 - odd, 1))
        buffer_b = jnp.where(hop == 1, 7, jnp.where(hop == 2, 1, nearby))
        side_b = jnp.where(hop == 1, 1, jnp.where(hop == 2, 0, odd))
        slot_b = jnp.where(hop == 3, 2 + 3 * odd, buffer_b)

        def pair(i, carry):
            step(
                jnp.where(i == 0, side_a, side_b), jnp.where(i == 0, buffer_a, buffer_b),
                jnp.where(i == 0, buffer_a, slot_b), chunk,
            )
            return carry

        lax.fori_loop(0, 2, pair, 0)
        return carry

    lax.fori_loop(0, 3 * chunks, rounds, 0)

    for copy in label_copies:
        copy.wait_send()
    for chunk in range(chunks):
        along(0, chunk).wait_send()
        along(1, chunk).wait_send()
        beside(chunk).wait_send()
    for piece in range(chunks + 1):
        first(0, piece).wait_send()
        first(1, piece).wait_send()

    def sent(hop):
        for down in range(2):
            for piece in range(chunks):
                onward(down, hop, piece).wait_send()

            @pl.when(is_short(down, hop) == 0)
            def _():
                onward(down, hop, chunks).wait_send()

    sent(1)
    sent(2)
    labels_arrive(0)
    labels_arrive(3)

    def ends(n, carry):
        side, chunk = lax.rem(n, 2), n // 2
        arrive_rows(3 * side, chunk)
        step(side, 3 * side, 3 * side, chunk)
        return carry

    lax.fori_loop(0, 2 * (chunks - 1), ends, 0)
    for side in range(2):
        arrive(3 * side, chunks - 1)
        arrive(3 * side, chunks)
        last[side] = held[3 * side, (chunks - 1) * ROWS :]
        marks[2 + side : 3 + side] = labels[3 * side, chunks - 1 :].astype(jnp.float32)
    sent(3)

    @pl.when(turned_at >= 0)
    def _():
        short_down().wait_send()


def finish_kernel(
    total, losses, columns, own, last, marks,
    loss_out, image_out, text_out,
    loss_ref, rounded, sems, loss_sem,
):
    chunks = own.shape[1] // ROWS
    t, b = marks[0:1], marks[1:2]
    wide_t = jnp.tile(t, (1, own.shape[2] // ROWS))
    copies = []
    both_sides = [
        pairs(own[side], last[side], columns[...], marks[2 + side : 3 + side], t, b) for side in range(2)
    ]
    for side, out in ((0, image_out), (1, text_out)):
        loss_all, coefficient_all = both_sides[side]
        for c in range(chunks):
            rows = pl.ds(c * ROWS, ROWS)
            loss = loss_all[c * ROWS : (c + 1) * ROWS]
            coefficient = coefficient_all[c * ROWS : (c + 1) * ROWS]
            grad = total[side, rows] + jnp.dot(coefficient, last[side], preferred_element_type=jnp.float32)
            rounded[side, rows] = (wide_t * grad).astype(jnp.bfloat16)
            copies.append(pltpu.make_async_copy(rounded.at[side, rows], out.at[rows], sems.at[side, c]))
            copies[-1].start()
            if side == 0:
                loss_ref[c : c + 1, :] = jnp.sum(
                    jnp.transpose(losses[0, rows] + loss), axis=0, keepdims=True
                ) * (1.0 / (4 * own.shape[1]))
        if side == 0:
            copies.append(pltpu.make_async_copy(loss_ref, loss_out, loss_sem))
            copies[-1].start()
    for copy in copies:
        copy.wait()


def per_device(groups, blocks, images, texts, row_pair_labels, logit_scale_log, logit_bias):
    rows, width = images.shape
    chunks = rows // ROWS
    pieces = chunks + 1
    vmem = pl.BlockSpec(memory_space=pltpu.VMEM)
    hbm = pl.BlockSpec(memory_space=pltpu.HBM)
    parts = pl.pallas_call(
        functools.partial(kernel, groups, blocks),
        out_shape=(
            pltpu.VMEM((2, rows, width), jnp.float32),
            pltpu.VMEM((2, rows, ROWS), jnp.float32),
            pltpu.VMEM((rows, ROWS), jnp.float32),
            pltpu.VMEM((2, rows, width), jnp.bfloat16),
            pltpu.VMEM((2, ROWS, width), jnp.bfloat16),
            pltpu.VMEM((8, ROWS), jnp.float32),
        ),
        in_specs=[pl.BlockSpec(memory_space=pltpu.SMEM)] * 2 + [hbm] * 3,
        out_specs=(vmem,) * 6,
        scratch_shapes=[
            pltpu.VMEM((15, rows, width), jnp.bfloat16),
            pltpu.VMEM((8, chunks, ROWS), jnp.int32),
            pltpu.SemaphoreType.DMA((4 + 2 * chunks,)),
            pltpu.SemaphoreType.DMA((12, pieces)),
            pltpu.SemaphoreType.DMA((15, pieces)),
            pltpu.SemaphoreType.DMA((6,)),
            pltpu.SemaphoreType.DMA((6,)),
            pltpu.SemaphoreType.REGULAR,
        ],
        compiler_params=pltpu.CompilerParams(
            collective_id=0, has_side_effects=True, vmem_limit_bytes=40 << 20
        ),
        cost_estimate=pl.CostEstimate(
            flops=32 * rows * rows * width, bytes_accessed=8 * rows * width, transcendentals=24 * rows * rows
        ),
    )(
        logit_scale_log,
        logit_bias,
        *(
            pltpu.with_memory_space_constraint(a, pltpu.HBM)
            for a in (row_pair_labels.reshape(chunks, ROWS), images, texts)
        ),
    )
    loss, image_grad, text_grad = pl.pallas_call(
        finish_kernel,
        out_shape=(
            jax.ShapeDtypeStruct((chunks, ROWS), jnp.float32),
            jax.ShapeDtypeStruct((rows, width), jnp.bfloat16),
            jax.ShapeDtypeStruct((rows, width), jnp.bfloat16),
        ),
        in_specs=[vmem] * 6,
        out_specs=(hbm,) * 3,
        scratch_shapes=[
            pltpu.VMEM((chunks, ROWS), jnp.float32),
            pltpu.VMEM((2, rows, width), jnp.bfloat16),
            pltpu.SemaphoreType.DMA((2, chunks)),
            pltpu.SemaphoreType.DMA,
        ],
        compiler_params=pltpu.CompilerParams(vmem_limit_bytes=24 << 20),
    )(*(pltpu.with_memory_space_constraint(a, pltpu.VMEM) for a in parts))
    return loss.reshape(rows), image_grad, text_grad


def solution(mesh):
    groups, blocks = mesh.shape["grp"], mesh.shape["blk"]
    both = P(("grp", "blk"))
    wide = P(("grp", "blk"), None)
    return jax.shard_map(
        functools.partial(per_device, groups, blocks),
        mesh=mesh,
        in_specs=(wide, wide, both, P(), P()),
        out_specs=(both, wide, wide),
        check_vma=False,
    )
```

```python
import functools
import jax
import jax.numpy as jnp
from jax import lax
from jax.experimental import pallas as pl
from jax.experimental.pallas import tpu as pltpu
from jax.sharding import PartitionSpec as P

MESH = pl.DeviceIdType.MESH
ROWS = 128
SPLIT = 64


def pairs(still, moving, still_labels, moving_labels, t, b):
    logit = t * lax.dot_general(
        still, moving, (((1,), (1,)), ((), ())), preferred_element_type=jnp.float32
    ) + b
    match = still_labels == moving_labels
    small = jnp.exp(-jnp.abs(logit))
    loss = jnp.maximum(logit, 0.0) + jnp.log1p(small) - jnp.where(match, logit, 0.0)
    gate = jnp.where(logit >= 0.0, 1.0, small) / (1.0 + small)
    return loss, (gate - jnp.where(match, 1.0, 0.0)).astype(jnp.bfloat16)


def kernel(
    groups, blocks,
    scale_ref, bias_ref, labels_in, images_ref, texts_ref,
    total, losses, columns, own, last, marks,
    held, labels,
    load_sem, send_sem, recv_sem, label_send, label_recv, ready, up_ready,
):
    g, k = lax.axis_index("grp"), lax.axis_index("blk")
    odd = lax.rem(g, 2)
    chunks = held.shape[1] // ROWS
    lows = groups // 2
    deep = 2 * lows

    def at(dg, dk):
        return (lax.rem(g + dg + groups, groups), lax.rem(k + dk + blocks, blocks))

    def world(w, place):
        return (place[0] + w * (groups - 1 - 2 * place[0]), place[1] + w * (blocks - 1 - 2 * place[1]))

    def height(place):
        return lows * lax.rem(place[1], 2) + place[0] // 2

    def on_chip(z, core, place):
        z = lax.rem(z + 2 * deep, deep)
        return (2 * lax.rem(z, lows) + core, place[1] - lax.rem(place[1], 2) + z // lows)

    z_here = height((g, k))
    top = deep - 1
    partner = (g + 1 - 2 * odd, k)
    barrier = pltpu.get_barrier_semaphore()
    for peer in (on_chip(z_here + 1, 0, (g, k)), partner):
        pl.semaphore_signal(barrier, inc=1, device_id=peer, device_id_type=MESH)

    @pl.when(z_here == 0)
    def _():
        pl.semaphore_signal(barrier, inc=1, device_id=on_chip(z_here - 1, 0, (g, k)), device_id_type=MESH)

    block_loads = [
        [
            pltpu.make_async_copy(
                source.at[pl.ds(chunk * ROWS, ROWS)], held.at[slot, pl.ds(chunk * ROWS, ROWS)],
                load_sem.at[4 + 2 * chunk + slot - 6],
            )
            for source, slot in ((texts_ref, 6), (images_ref, 7))
        ]
        for chunk in range(chunks)
    ]
    for pair in block_loads:
        for load in pair:
            load.start()

    def inner(z):
        return jnp.where(lax.rem(z + 2 * deep, lows) < lows - 1, 1, 0)

    def way(place):
        return jnp.where(lax.rem(place[0], 2) == inner(place[0] // 2), 0, 1)

    def core_of(z, down):
        return inner(z) + down * (1 - 2 * inner(z))

    mine = world(odd, (g, k))
    z = height(mine)

    def moved(place, yes):
        return (place[0], lax.rem(place[1] + 2 * yes + blocks, blocks))

    def turns(down, hop, source):
        source = lax.rem(source + 2 * deep, deep)
        if down == 0:
            return jnp.where(hop == 1, source // lows, 0)
        return jnp.where(hop == 3 - inner(source), source // lows, 0)

    def goes_to(down, hop):
        up = 1 - 2 * down
        source = z - hop * up
        core = jnp.where(hop == 3, core_of(source, down), 0)
        return world(odd, moved(on_chip(z + up, core, mine), turns(down, hop, source)))

    def first_to(w):
        place = world(w, (g, k))
        down = way(place)
        return world(w, on_chip(height(place) + 1 - 2 * down, 0, place)), down

    targets = [at(0, 1), at(0, 2), at(1, 0), at(0, -1), at(0, -2), at(-1, 0)]
    text_first, text_down = first_to(0)
    image_first, image_down = first_to(1)
    low = g // 2
    far = [
        moved(on_chip(z_here + up, 1, (g, k)), side) for side in (-1, 1) for up in (-1, 0, 1)
    ] + [(2 * low + 1, at(0, 1)[1]), (2 * low + 1, at(0, -1)[1]), (2 * (lows - 1 - low) + 1, k)]
    loads = [
        pltpu.make_async_copy(labels_in, labels.at[6], load_sem.at[2]),
        pltpu.make_async_copy(labels_in, labels.at[7], load_sem.at[3]),
    ]
    def wait_below():
        @pl.when(odd == 0)
        def _():
            pl.semaphore_wait(barrier, jnp.where(z_here == top, 5, 3))
            pl.semaphore_signal(ready, inc=1, device_id=partner, device_id_type=MESH)

            @pl.when(z_here > 0)
            def _():
                for core in range(2):
                    below = on_chip(z_here - 1, core, (g, k))
                    pl.semaphore_signal(up_ready, inc=1, device_id=below, device_id_type=MESH)

        @pl.when(odd == 1)
        def _():
            pl.semaphore_wait(ready, 1)

    def wait_above():
        @pl.when(z_here < top)
        def _():
            pl.semaphore_wait(up_ready, 1)

    tail = chunks * ROWS - SPLIT

    def rows_of(piece):
        if isinstance(piece, int) and piece >= chunks - 1:
            return pl.ds(tail, SPLIT) if piece == chunks else pl.ds((chunks - 1) * ROWS, ROWS - SPLIT)
        return pl.ds(pl.multiple_of(piece * ROWS, ROWS), ROWS)

    def block_copy(source, slot, piece, flow, device):
        rows = rows_of(piece)
        return pltpu.make_async_remote_copy(
            src_ref=source.at[rows], dst_ref=held.at[slot, rows],
            send_sem=send_sem.at[flow, piece], recv_sem=recv_sem.at[slot, piece],
            device_id=device, device_id_type=MESH,
        )

    def whole_copy(source, slot, chunk, flow, device):
        rows = pl.ds(chunk * ROWS, ROWS)
        return pltpu.make_async_remote_copy(
            src_ref=source.at[rows], dst_ref=held.at[slot, rows],
            send_sem=send_sem.at[flow, chunk], recv_sem=recv_sem.at[slot, chunk],
            device_id=device, device_id_type=MESH,
        )

    rising = jnp.where(z_here < lows, 1, 0)
    passed = jnp.where(rising == 1, z_here, top - z_here)
    turns_now = jnp.where(passed == lows - 1, jnp.where(rising == 1, odd, 1 - odd), 0)
    turned_to = world(odd, moved(on_chip(z + (2 * rising - 1) * (1 - 2 * odd), 0, mine), turns_now))

    def first(w, piece):
        source, down, device = [(6, text_down, text_first), (7, image_down, image_first)][w]
        slot = 8 + 3 * down
        if piece == chunks:
            turned = jnp.where(odd == w, jnp.where(passed == 0, 1, 0), 0)
            slot = jnp.where(turned == 1, 14, slot)
            device = tuple(jnp.where(turned == 1, x, y) for x, y in zip(turned_to, device))
        return block_copy(held.at[source], slot, piece, w, device)

    def turned_on():
        slot = jnp.where(passed == lows - 1, 3 * odd, 14)
        return block_copy(held.at[14], slot, chunks, 11, turned_to)

    def along(w, chunk):
        if w == 0:
            return whole_copy(held.at[6], 1, chunk, 2, targets[1])
        return whole_copy(held.at[7], 4, chunk, 3, targets[4])

    def beside(chunk):
        return whole_copy(held.at[6 + odd], 2 + 3 * odd, chunk, 4, partner)

    def onward(down, hop, piece):
        buffer = 7 + 3 * down + hop
        slot = jnp.where(hop == 3, 3 * odd, buffer + 1)
        return block_copy(held.at[buffer], slot, piece, 4 + 3 * down + hop, goes_to(down, hop))

    def is_short(down, hop):
        return jnp.where(hop == jnp.where(odd == down, z_here + 1, deep - z_here), 1, 0)

    label_copies = [
        pltpu.make_async_remote_copy(
            src_ref=labels_in, dst_ref=labels.at[slot],
            send_sem=label_send.at[slot], recv_sem=label_recv.at[slot],
            device_id=targets[slot], device_id_type=MESH,
        )
        for slot in range(6)
    ]

    def send_first(falling):
        for w, falls in ((0, text_down), (1, 1 - image_down)):
            @pl.when(falls == falling)
            def _():
                for chunk in range(chunks):
                    block_loads[chunk][w].wait()
                    first(w, chunk).start()
                first(w, chunks).start()

    lowest = jnp.where(z_here == 0, 1, 0)
    pl.when(lowest == 0)(wait_below)
    pl.when(lowest == 1)(wait_above)
    send_first(1 - lowest)
    pl.when(lowest == 0)(wait_above)
    pl.when(lowest == 1)(wait_below)
    send_first(lowest)
    for peer in far:
        pl.semaphore_signal(barrier, inc=1, device_id=peer, device_id_type=MESH)
    for load in loads:
        load.start()

    @pl.when(odd == 1)
    def _():
        pl.semaphore_wait(barrier, 2 * len(far) + 1)
        pl.semaphore_signal(ready, inc=1, device_id=partner, device_id_type=MESH)

    @pl.when(odd == 0)
    def _():
        pl.semaphore_wait(ready, 1)

    for copy in label_copies:
        copy.start()
    for chunk in range(chunks):
        along(0, chunk).start()
        along(1, chunk).start()
    for load in loads:
        load.wait()
    for chunk in range(chunks):
        beside(chunk).start()

    t = jnp.exp(jnp.full((1, ROWS), scale_ref[0], jnp.float32))
    b = jnp.full((1, ROWS), bias_ref[0], jnp.float32)
    for c in range(chunks):
        row = labels[6, c : c + 1, :].astype(jnp.float32)
        columns[c * ROWS : (c + 1) * ROWS] = jnp.transpose(jnp.broadcast_to(row, (ROWS, ROWS)))
    total[...] = jnp.zeros_like(total)
    losses[...] = jnp.zeros_like(losses)

    marks[0:1] = t
    marks[1:2] = b
    for side in range(2):
        own[side] = held[7 - side]

    def step(side, buffer, slot, chunk):
        rows = pl.ds(pl.multiple_of(chunk * ROWS, ROWS), ROWS)
        moving = held[buffer, rows]
        loss, coefficient = pairs(
            held[7 - side], moving, columns[...], labels[slot, pl.ds(chunk, 1)].astype(jnp.float32), t, b
        )
        losses[side] += loss
        total[side] += jnp.dot(coefficient, moving, preferred_element_type=jnp.float32)

    def arrive(slot, piece):
        rows = rows_of(piece)
        pltpu.make_async_copy(held.at[slot, rows], held.at[slot, rows], recv_sem.at[slot, piece]).wait()

    def arrive_rows(slot, chunk):
        rows = pl.ds(pl.multiple_of(chunk * ROWS, ROWS), ROWS)
        pltpu.make_async_copy(held.at[slot, rows], held.at[slot, rows], recv_sem.at[slot, chunk]).wait()

    def pass_on(hop, chunk):
        for down in range(2):
            @pl.when(chunk < chunks - 1)
            def _():
                arrive(7 + 3 * down + hop, chunk)
                onward(down, hop, chunk).start()

            @pl.when(chunk == chunks - 1)
            def _():
                arrive(7 + 3 * down + hop, chunks - 1)
                onward(down, hop, chunks - 1).start()

                @pl.when(is_short(down, hop) == 0)
                def _():
                    arrive(7 + 3 * down + hop, chunks)
                    onward(down, hop, chunks).start()

    turned_at = jnp.where(
        passed == 1, chunks, jnp.where(passed == 2, 2 * chunks, jnp.where(passed == 3, 3 * chunks - 1, -1))
    )

    near = 5 - 3 * odd
    nearby = 8 + jnp.where(mine[0] == 0, 5, 0)

    def labels_arrive(slot):
        pltpu.make_async_copy(labels.at[slot], labels.at[slot], label_recv.at[slot]).wait()

    def rounds(n, carry):
        hop, chunk = n // chunks + 1, lax.rem(n, chunks)
        pass_on(hop, chunk)

        @pl.when(n == turned_at)
        def _():
            arrive(14, chunks)
            turned_on().start()

        @pl.when(n == chunks)
        def _():
            labels_arrive(near)
            labels_arrive(1)

        @pl.when(n == 2 * chunks)
        def _():
            labels_arrive(4)
            labels_arrive(2 + 3 * odd)

        @pl.when(hop == 2)
        def _():
            arrive_rows(near, chunk)
            arrive_rows(1, chunk)

        @pl.when(hop == 3)
        def _():
            arrive_rows(4, chunk)

        buffer_a = jnp.where(hop == 1, 6, jnp.where(hop == 2, near, 4))
        side_a = jnp.where(hop == 1, 0, jnp.where(hop == 2, 1 - odd, 1))
        buffer_b = jnp.where(hop == 1, 7, jnp.where(hop == 2, 1, nearby))
        side_b = jnp.where(hop == 1, 1, jnp.where(hop == 2, 0, odd))
        slot_b = jnp.where(hop == 3, 2 + 3 * odd, buffer_b)

        def pair(i, carry):
            step(
                jnp.where(i == 0, side_a, side_b), jnp.where(i == 0, buffer_a, buffer_b),
                jnp.where(i == 0, buffer_a, slot_b), chunk,
            )
            return carry

        lax.fori_loop(0, 2, pair, 0)
        return carry

    lax.fori_loop(0, 3 * chunks, rounds, 0)

    for copy in label_copies:
        copy.wait_send()
    for chunk in range(chunks):
        along(0, chunk).wait_send()
        along(1, chunk).wait_send()
        beside(chunk).wait_send()
    for piece in range(chunks + 1):
        first(0, piece).wait_send()
        first(1, piece).wait_send()

    def sent(hop):
        for down in range(2):
            for piece in range(chunks):
                onward(down, hop, piece).wait_send()

            @pl.when(is_short(down, hop) == 0)
            def _():
                onward(down, hop, chunks).wait_send()

    sent(1)
    sent(2)
    labels_arrive(0)
    labels_arrive(3)

    def ends(n, carry):
        side, chunk = lax.rem(n, 2), n // 2
        arrive_rows(3 * side, chunk)
        step(side, 3 * side, 3 * side, chunk)
        return carry

    lax.fori_loop(0, 2 * (chunks - 1), ends, 0)
    for side in range(2):
        arrive(3 * side, chunks - 1)
        arrive(3 * side, chunks)
        last[side] = held[3 * side, (chunks - 1) * ROWS :]
        marks[2 + side : 3 + side] = labels[3 * side, chunks - 1 :].astype(jnp.float32)
    sent(3)

    @pl.when(turned_at >= 0)
    def _():
        turned_on().wait_send()


def finish_kernel(
    total, losses, columns, own, last, marks,
    loss_out, image_out, text_out,
    loss_ref, rounded, sems, loss_sem,
):
    chunks = own.shape[1] // ROWS
    t, b = marks[0:1], marks[1:2]
    wide_t = jnp.tile(t, (1, own.shape[2] // ROWS))
    copies = []
    both_sides = [
        pairs(own[side], last[side], columns[...], marks[2 + side : 3 + side], t, b) for side in range(2)
    ]
    for side, out in ((0, image_out), (1, text_out)):
        loss_all, coefficient_all = both_sides[side]
        for c in range(chunks):
            rows = pl.ds(c * ROWS, ROWS)
            loss = loss_all[c * ROWS : (c + 1) * ROWS]
            coefficient = coefficient_all[c * ROWS : (c + 1) * ROWS]
            grad = total[side, rows] + jnp.dot(coefficient, last[side], preferred_element_type=jnp.float32)
            rounded[side, rows] = (wide_t * grad).astype(jnp.bfloat16)
            copies.append(pltpu.make_async_copy(rounded.at[side, rows], out.at[rows], sems.at[side, c]))
            copies[-1].start()
            if side == 0:
                loss_ref[c : c + 1, :] = jnp.sum(
                    jnp.transpose(losses[0, rows] + loss), axis=0, keepdims=True
                ) * (1.0 / (4 * own.shape[1]))
        if side == 0:
            copies.append(pltpu.make_async_copy(loss_ref, loss_out, loss_sem))
            copies[-1].start()
    for copy in copies:
        copy.wait()


def per_device(groups, blocks, images, texts, row_pair_labels, logit_scale_log, logit_bias):
    rows, width = images.shape
    chunks = rows // ROWS
    pieces = chunks + 1
    vmem = pl.BlockSpec(memory_space=pltpu.VMEM)
    hbm = pl.BlockSpec(memory_space=pltpu.HBM)
    parts = pl.pallas_call(
        functools.partial(kernel, groups, blocks),
        out_shape=(
            pltpu.VMEM((2, rows, width), jnp.float32),
            pltpu.VMEM((2, rows, ROWS), jnp.float32),
            pltpu.VMEM((rows, ROWS), jnp.float32),
            pltpu.VMEM((2, rows, width), jnp.bfloat16),
            pltpu.VMEM((2, ROWS, width), jnp.bfloat16),
            pltpu.VMEM((8, ROWS), jnp.float32),
        ),
        in_specs=[pl.BlockSpec(memory_space=pltpu.SMEM)] * 2 + [hbm] * 3,
        out_specs=(vmem,) * 6,
        scratch_shapes=[
            pltpu.VMEM((15, rows, width), jnp.bfloat16),
            pltpu.VMEM((8, chunks, ROWS), jnp.int32),
            pltpu.SemaphoreType.DMA((4 + 2 * chunks,)),
            pltpu.SemaphoreType.DMA((12, pieces)),
            pltpu.SemaphoreType.DMA((15, pieces)),
            pltpu.SemaphoreType.DMA((6,)),
            pltpu.SemaphoreType.DMA((6,)),
            pltpu.SemaphoreType.REGULAR,
            pltpu.SemaphoreType.REGULAR,
        ],
        compiler_params=pltpu.CompilerParams(
            collective_id=0, has_side_effects=True, vmem_limit_bytes=40 << 20
        ),
        cost_estimate=pl.CostEstimate(
            flops=32 * rows * rows * width, bytes_accessed=8 * rows * width, transcendentals=24 * rows * rows
        ),
    )(
        logit_scale_log,
        logit_bias,
        *(
            pltpu.with_memory_space_constraint(a, pltpu.HBM)
            for a in (row_pair_labels.reshape(chunks, ROWS), images, texts)
        ),
    )
    loss, image_grad, text_grad = pl.pallas_call(
        finish_kernel,
        out_shape=(
            jax.ShapeDtypeStruct((chunks, ROWS), jnp.float32),
            jax.ShapeDtypeStruct((rows, width), jnp.bfloat16),
            jax.ShapeDtypeStruct((rows, width), jnp.bfloat16),
        ),
        in_specs=[vmem] * 6,
        out_specs=(hbm,) * 3,
        scratch_shapes=[
            pltpu.VMEM((chunks, ROWS), jnp.float32),
            pltpu.VMEM((2, rows, width), jnp.bfloat16),
            pltpu.SemaphoreType.DMA((2, chunks)),
            pltpu.SemaphoreType.DMA,
        ],
        compiler_params=pltpu.CompilerParams(vmem_limit_bytes=24 << 20),
    )(*(pltpu.with_memory_space_constraint(a, pltpu.VMEM) for a in parts))
    return loss.reshape(rows), image_grad, text_grad


def solution(mesh):
    groups, blocks = mesh.shape["grp"], mesh.shape["blk"]
    both = P(("grp", "blk"))
    wide = P(("grp", "blk"), None)
    return jax.shard_map(
        functools.partial(per_device, groups, blocks),
        mesh=mesh,
        in_specs=(wide, wide, both, P(), P()),
        out_specs=(both, wide, wide),
        check_vma=False,
    )
```

```python
import functools
import jax
import jax.numpy as jnp
from jax import lax
from jax.experimental import pallas as pl
from jax.experimental.pallas import tpu as pltpu
from jax.sharding import PartitionSpec as P

MESH = pl.DeviceIdType.MESH
ROWS = 128
SPLIT = 48


def pairs(still, moving, still_labels, moving_labels, t, b):
    logit = t * lax.dot_general(
        still, moving, (((1,), (1,)), ((), ())), preferred_element_type=jnp.float32
    ) + b
    match = still_labels == moving_labels
    small = jnp.exp(-jnp.abs(logit))
    loss = jnp.maximum(logit, 0.0) + jnp.log1p(small) - jnp.where(match, logit, 0.0)
    gate = jnp.where(logit >= 0.0, 1.0, small) / (1.0 + small)
    return loss, (gate - jnp.where(match, 1.0, 0.0)).astype(jnp.bfloat16)


def kernel(
    groups, blocks,
    scale_ref, bias_ref, labels_in, images_ref, texts_ref,
    total, losses, columns, own, last, marks,
    held, labels,
    load_sem, send_sem, recv_sem, label_send, label_recv, ready, up_ready,
):
    g, k = lax.axis_index("grp"), lax.axis_index("blk")
    odd = lax.rem(g, 2)
    chunks = held.shape[1] // ROWS
    lows = groups // 2
    deep = 2 * lows

    def at(dg, dk):
        return (lax.rem(g + dg + groups, groups), lax.rem(k + dk + blocks, blocks))

    def world(w, place):
        return (place[0] + w * (groups - 1 - 2 * place[0]), place[1] + w * (blocks - 1 - 2 * place[1]))

    def height(place):
        return lows * lax.rem(place[1], 2) + place[0] // 2

    def on_chip(z, core, place):
        z = lax.rem(z + 2 * deep, deep)
        return (2 * lax.rem(z, lows) + core, place[1] - lax.rem(place[1], 2) + z // lows)

    z_here = height((g, k))
    top = deep - 1
    partner = (g + 1 - 2 * odd, k)
    barrier = pltpu.get_barrier_semaphore()
    for peer in (on_chip(z_here + 1, 0, (g, k)), partner):
        pl.semaphore_signal(barrier, inc=1, device_id=peer, device_id_type=MESH)

    @pl.when(z_here == 0)
    def _():
        pl.semaphore_signal(barrier, inc=1, device_id=on_chip(z_here - 1, 0, (g, k)), device_id_type=MESH)

    block_loads = [
        [
            pltpu.make_async_copy(
                source.at[pl.ds(chunk * ROWS, ROWS)], held.at[slot, pl.ds(chunk * ROWS, ROWS)],
                load_sem.at[4 + 2 * chunk + slot - 6],
            )
            for source, slot in ((texts_ref, 6), (images_ref, 7))
        ]
        for chunk in range(chunks)
    ]
    for pair in block_loads:
        for load in pair:
            load.start()

    def inner(z):
        return jnp.where(lax.rem(z + 2 * deep, lows) < lows - 1, 1, 0)

    def way(place):
        return jnp.where(lax.rem(place[0], 2) == inner(place[0] // 2), 0, 1)

    def core_of(z, down):
        return inner(z) + down * (1 - 2 * inner(z))

    mine = world(odd, (g, k))
    z = height(mine)

    def moved(place, yes):
        return (place[0], lax.rem(place[1] + 2 * yes + blocks, blocks))

    def turns(down, hop, source):
        source = lax.rem(source + 2 * deep, deep)
        at_hop = jnp.where(down == 0, 1, 3 - inner(source))
        return jnp.where(hop == at_hop, source // lows, 0)

    def goes_to(down, hop):
        up = 1 - 2 * down
        source = z - hop * up
        core = jnp.where(hop == 3, core_of(source, down), 0)
        return world(odd, moved(on_chip(z + up, core, mine), turns(down, hop, source)))

    def first_to(w):
        place = world(w, (g, k))
        down = way(place)
        return world(w, on_chip(height(place) + 1 - 2 * down, 0, place)), down

    targets = [at(0, 1), at(0, 2), at(1, 0), at(0, -1), at(0, -2), at(-1, 0)]
    text_first, text_down = first_to(0)
    image_first, image_down = first_to(1)
    low = g // 2
    far = [
        moved(on_chip(z_here + up, 1, (g, k)), side) for side in (-1, 1) for up in (-1, 0, 1)
    ] + [(2 * low + 1, at(0, 1)[1]), (2 * low + 1, at(0, -1)[1]), (2 * (lows - 1 - low) + 1, k)]
    loads = [
        pltpu.make_async_copy(labels_in, labels.at[6], load_sem.at[2]),
        pltpu.make_async_copy(labels_in, labels.at[7], load_sem.at[3]),
    ]
    def wait_below():
        @pl.when(odd == 0)
        def _():
            pl.semaphore_wait(barrier, jnp.where(z_here == top, 5, 3))
            pl.semaphore_signal(ready, inc=1, device_id=partner, device_id_type=MESH)

            @pl.when(z_here > 0)
            def _():
                for core in range(2):
                    below = on_chip(z_here - 1, core, (g, k))
                    pl.semaphore_signal(up_ready, inc=1, device_id=below, device_id_type=MESH)

        @pl.when(odd == 1)
        def _():
            pl.semaphore_wait(ready, 1)

    def wait_above():
        @pl.when(z_here < top)
        def _():
            pl.semaphore_wait(up_ready, 1)

    tail = chunks * ROWS - SPLIT

    def rows_of(piece):
        if isinstance(piece, int) and piece >= chunks - 1:
            return pl.ds(tail, SPLIT) if piece == chunks else pl.ds((chunks - 1) * ROWS, ROWS - SPLIT)
        return pl.ds(pl.multiple_of(piece * ROWS, ROWS), ROWS)

    def block_copy(source, slot, piece, flow, device):
        rows = rows_of(piece)
        return pltpu.make_async_remote_copy(
            src_ref=source.at[rows], dst_ref=held.at[slot, rows],
            send_sem=send_sem.at[flow, piece], recv_sem=recv_sem.at[slot, piece],
            device_id=device, device_id_type=MESH,
        )

    def whole_copy(source, slot, chunk, flow, device):
        rows = pl.ds(chunk * ROWS, ROWS)
        return pltpu.make_async_remote_copy(
            src_ref=source.at[rows], dst_ref=held.at[slot, rows],
            send_sem=send_sem.at[flow, chunk], recv_sem=recv_sem.at[slot, chunk],
            device_id=device, device_id_type=MESH,
        )

    rising = jnp.where(z_here < lows, 1, 0)
    passed = jnp.where(rising == 1, z_here, top - z_here)
    turns_now = jnp.where(passed == lows - 1, jnp.where(rising == 1, odd, 1 - odd), 0)
    turned_to = world(odd, moved(on_chip(z + (2 * rising - 1) * (1 - 2 * odd), 0, mine), turns_now))

    def first(w, piece):
        source, down, device = [(6, text_down, text_first), (7, image_down, image_first)][w]
        slot = 8 + 3 * down
        if piece == chunks:
            turned = jnp.where(odd == w, jnp.where(passed == 0, 1, 0), 0)
            slot = jnp.where(turned == 1, 14, slot)
            device = tuple(jnp.where(turned == 1, x, y) for x, y in zip(turned_to, device))
        return block_copy(held.at[source], slot, piece, w, device)

    def turned_on():
        slot = jnp.where(passed == lows - 1, 3 * odd, 14)
        return block_copy(held.at[14], slot, chunks, 11, turned_to)

    def along(w, chunk):
        if w == 0:
            return whole_copy(held.at[6], 1, chunk, 2, targets[1])
        return whole_copy(held.at[7], 4, chunk, 3, targets[4])

    def beside(chunk):
        return whole_copy(held.at[6 + odd], 2 + 3 * odd, chunk, 4, partner)

    def onward(down, hop, piece):
        buffer = 7 + 3 * down + hop
        slot = jnp.where(hop == 3, 3 * odd, buffer + 1)
        return block_copy(held.at[buffer], slot, piece, 4 + 3 * down + hop, goes_to(down, hop))

    def is_short(down, hop):
        return jnp.where(hop == jnp.where(odd == down, z_here + 1, deep - z_here), 1, 0)

    label_copies = [
        pltpu.make_async_remote_copy(
            src_ref=labels_in, dst_ref=labels.at[slot],
            send_sem=label_send.at[slot], recv_sem=label_recv.at[slot],
            device_id=targets[slot], device_id_type=MESH,
        )
        for slot in range(6)
    ]

    def send_first(falling):
        for w, falls in ((0, text_down), (1, 1 - image_down)):
            @pl.when(falls == falling)
            def _():
                for chunk in range(chunks):
                    block_loads[chunk][w].wait()
                    first(w, chunk).start()
                first(w, chunks).start()

    lowest = jnp.where(z_here == 0, 1, 0)
    pl.when(lowest == 0)(wait_below)
    pl.when(lowest == 1)(wait_above)
    send_first(1 - lowest)
    pl.when(lowest == 0)(wait_above)
    pl.when(lowest == 1)(wait_below)
    send_first(lowest)
    for peer in far:
        pl.semaphore_signal(barrier, inc=1, device_id=peer, device_id_type=MESH)
    for load in loads:
        load.start()

    @pl.when(odd == 1)
    def _():
        pl.semaphore_wait(barrier, 2 * len(far) + 1)
        pl.semaphore_signal(ready, inc=1, device_id=partner, device_id_type=MESH)

    @pl.when(odd == 0)
    def _():
        pl.semaphore_wait(ready, 1)

    for copy in label_copies:
        copy.start()
    for chunk in range(chunks):
        along(0, chunk).start()
        along(1, chunk).start()
    for load in loads:
        load.wait()
    for chunk in range(chunks):
        beside(chunk).start()

    t = jnp.exp(jnp.full((1, ROWS), scale_ref[0], jnp.float32))
    b = jnp.full((1, ROWS), bias_ref[0], jnp.float32)
    for c in range(chunks):
        row = labels[6, c : c + 1, :].astype(jnp.float32)
        columns[c * ROWS : (c + 1) * ROWS] = jnp.transpose(jnp.broadcast_to(row, (ROWS, ROWS)))
    total[...] = jnp.zeros_like(total)
    losses[...] = jnp.zeros_like(losses)

    marks[0:1] = t
    marks[1:2] = b
    for side in range(2):
        own[side] = held[7 - side]

    def step(side, buffer, slot, chunk):
        rows = pl.ds(pl.multiple_of(chunk * ROWS, ROWS), ROWS)
        moving = held[buffer, rows]
        loss, coefficient = pairs(
            held[7 - side], moving, columns[...], labels[slot, pl.ds(chunk, 1)].astype(jnp.float32), t, b
        )
        losses[side] += loss
        total[side] += jnp.dot(coefficient, moving, preferred_element_type=jnp.float32)

    def arrive(slot, piece):
        rows = rows_of(piece)
        pltpu.make_async_copy(held.at[slot, rows], held.at[slot, rows], recv_sem.at[slot, piece]).wait()

    def arrive_rows(slot, chunk):
        rows = pl.ds(pl.multiple_of(chunk * ROWS, ROWS), ROWS)
        pltpu.make_async_copy(held.at[slot, rows], held.at[slot, rows], recv_sem.at[slot, chunk]).wait()

    early = jnp.where(z_here < lows - 1, 1 - odd, odd)

    def pass_on(down, n):
        hop, chunk = n // chunks + 1, lax.rem(n, chunks)

        @pl.when(chunk < chunks - 1)
        def _():
            arrive(7 + 3 * down + hop, chunk)
            onward(down, hop, chunk).start()

        @pl.when(chunk == chunks - 1)
        def _():
            arrive(7 + 3 * down + hop, chunks - 1)
            onward(down, hop, chunks - 1).start()

            @pl.when(is_short(down, hop) == 0)
            def _():
                arrive(7 + 3 * down + hop, chunks)
                onward(down, hop, chunks).start()

    turned_at = jnp.where(
        passed == 1, chunks, jnp.where(passed == 2, 2 * chunks, jnp.where(passed == 3, 3 * chunks - 1, -1))
    )

    near = 5 - 3 * odd
    nearby = 8 + jnp.where(mine[0] == 0, 5, 0)

    def labels_arrive(slot):
        pltpu.make_async_copy(labels.at[slot], labels.at[slot], label_recv.at[slot]).wait()

    def rounds(n, carry):
        hop, chunk = n // chunks + 1, lax.rem(n, chunks)
        pass_on(1 - early, n)

        @pl.when(n < 3 * chunks - 1)
        def _():
            pass_on(early, n + 1)

        @pl.when(n == turned_at)
        def _():
            arrive(14, chunks)
            turned_on().start()

        @pl.when(n == chunks)
        def _():
            labels_arrive(near)
            labels_arrive(1)

        @pl.when(n == 2 * chunks)
        def _():
            labels_arrive(4)
            labels_arrive(2 + 3 * odd)

        @pl.when(hop == 2)
        def _():
            arrive_rows(near, chunk)
            arrive_rows(1, chunk)

        @pl.when(hop == 3)
        def _():
            arrive_rows(4, chunk)

        buffer_a = jnp.where(hop == 1, 6, jnp.where(hop == 2, near, 4))
        side_a = jnp.where(hop == 1, 0, jnp.where(hop == 2, 1 - odd, 1))
        buffer_b = jnp.where(hop == 1, 7, jnp.where(hop == 2, 1, nearby))
        side_b = jnp.where(hop == 1, 1, jnp.where(hop == 2, 0, odd))
        slot_b = jnp.where(hop == 3, 2 + 3 * odd, buffer_b)

        def pair(i, carry):
            step(
                jnp.where(i == 0, side_a, side_b), jnp.where(i == 0, buffer_a, buffer_b),
                jnp.where(i == 0, buffer_a, slot_b), chunk,
            )
            return carry

        lax.fori_loop(0, 2, pair, 0)
        return carry

    pass_on(early, 0)
    lax.fori_loop(0, 3 * chunks, rounds, 0)

    for copy in label_copies:
        copy.wait_send()
    for chunk in range(chunks):
        along(0, chunk).wait_send()
        along(1, chunk).wait_send()
        beside(chunk).wait_send()
    for piece in range(chunks + 1):
        first(0, piece).wait_send()
        first(1, piece).wait_send()

    def sent(hop):
        for down in range(2):
            for piece in range(chunks):
                onward(down, hop, piece).wait_send()

            @pl.when(is_short(down, hop) == 0)
            def _():
                onward(down, hop, chunks).wait_send()

    sent(1)
    sent(2)
    labels_arrive(0)
    labels_arrive(3)

    def ends(n, carry):
        side, chunk = lax.rem(n, 2), n // 2
        arrive_rows(3 * side, chunk)
        step(side, 3 * side, 3 * side, chunk)
        return carry

    lax.fori_loop(0, 2 * (chunks - 1), ends, 0)
    for side in range(2):
        arrive(3 * side, chunks - 1)
        arrive(3 * side, chunks)
        last[side] = held[3 * side, (chunks - 1) * ROWS :]
        marks[2 + side : 3 + side] = labels[3 * side, chunks - 1 :].astype(jnp.float32)
    sent(3)

    @pl.when(turned_at >= 0)
    def _():
        turned_on().wait_send()


def finish_kernel(
    total, losses, columns, own, last, marks,
    loss_out, image_out, text_out,
    loss_ref, rounded, sems, loss_sem,
):
    chunks = own.shape[1] // ROWS
    t, b = marks[0:1], marks[1:2]
    wide_t = jnp.tile(t, (1, own.shape[2] // ROWS))
    copies = []
    both_sides = [
        pairs(own[side], last[side], columns[...], marks[2 + side : 3 + side], t, b) for side in range(2)
    ]
    for side, out in ((0, image_out), (1, text_out)):
        loss_all, coefficient_all = both_sides[side]
        for c in range(chunks):
            rows = pl.ds(c * ROWS, ROWS)
            loss = loss_all[c * ROWS : (c + 1) * ROWS]
            coefficient = coefficient_all[c * ROWS : (c + 1) * ROWS]
            grad = total[side, rows] + jnp.dot(coefficient, last[side], preferred_element_type=jnp.float32)
            rounded[side, rows] = (wide_t * grad).astype(jnp.bfloat16)
            copies.append(pltpu.make_async_copy(rounded.at[side, rows], out.at[rows], sems.at[side, c]))
            copies[-1].start()
            if side == 0:
                loss_ref[c : c + 1, :] = jnp.sum(
                    jnp.transpose(losses[0, rows] + loss), axis=0, keepdims=True
                ) * (1.0 / (4 * own.shape[1]))
        if side == 0:
            copies.append(pltpu.make_async_copy(loss_ref, loss_out, loss_sem))
            copies[-1].start()
    for copy in copies:
        copy.wait()


def per_device(groups, blocks, images, texts, row_pair_labels, logit_scale_log, logit_bias):
    rows, width = images.shape
    chunks = rows // ROWS
    pieces = chunks + 1
    vmem = pl.BlockSpec(memory_space=pltpu.VMEM)
    hbm = pl.BlockSpec(memory_space=pltpu.HBM)
    parts = pl.pallas_call(
        functools.partial(kernel, groups, blocks),
        out_shape=(
            pltpu.VMEM((2, rows, width), jnp.float32),
            pltpu.VMEM((2, rows, ROWS), jnp.float32),
            pltpu.VMEM((rows, ROWS), jnp.float32),
            pltpu.VMEM((2, rows, width), jnp.bfloat16),
            pltpu.VMEM((2, ROWS, width), jnp.bfloat16),
            pltpu.VMEM((8, ROWS), jnp.float32),
        ),
        in_specs=[pl.BlockSpec(memory_space=pltpu.SMEM)] * 2 + [hbm] * 3,
        out_specs=(vmem,) * 6,
        scratch_shapes=[
            pltpu.VMEM((15, rows, width), jnp.bfloat16),
            pltpu.VMEM((8, chunks, ROWS), jnp.int32),
            pltpu.SemaphoreType.DMA((4 + 2 * chunks,)),
            pltpu.SemaphoreType.DMA((12, pieces)),
            pltpu.SemaphoreType.DMA((15, pieces)),
            pltpu.SemaphoreType.DMA((6,)),
            pltpu.SemaphoreType.DMA((6,)),
            pltpu.SemaphoreType.REGULAR,
            pltpu.SemaphoreType.REGULAR,
        ],
        compiler_params=pltpu.CompilerParams(
            collective_id=0, has_side_effects=True, vmem_limit_bytes=40 << 20
        ),
        cost_estimate=pl.CostEstimate(
            flops=32 * rows * rows * width, bytes_accessed=8 * rows * width, transcendentals=24 * rows * rows
        ),
    )(
        logit_scale_log,
        logit_bias,
        *(
            pltpu.with_memory_space_constraint(a, pltpu.HBM)
            for a in (row_pair_labels.reshape(chunks, ROWS), images, texts)
        ),
    )
    loss, image_grad, text_grad = pl.pallas_call(
        finish_kernel,
        out_shape=(
            jax.ShapeDtypeStruct((chunks, ROWS), jnp.float32),
            jax.ShapeDtypeStruct((rows, width), jnp.bfloat16),
            jax.ShapeDtypeStruct((rows, width), jnp.bfloat16),
        ),
        in_specs=[vmem] * 6,
        out_specs=(hbm,) * 3,
        scratch_shapes=[
            pltpu.VMEM((chunks, ROWS), jnp.float32),
            pltpu.VMEM((2, rows, width), jnp.bfloat16),
            pltpu.SemaphoreType.DMA((2, chunks)),
            pltpu.SemaphoreType.DMA,
        ],
        compiler_params=pltpu.CompilerParams(vmem_limit_bytes=24 << 20),
    )(*(pltpu.with_memory_space_constraint(a, pltpu.VMEM) for a in parts))
    return loss.reshape(rows), image_grad, text_grad


def solution(mesh):
    groups, blocks = mesh.shape["grp"], mesh.shape["blk"]
    both = P(("grp", "blk"))
    wide = P(("grp", "blk"), None)
    return jax.shard_map(
        functools.partial(per_device, groups, blocks),
        mesh=mesh,
        in_specs=(wide, wide, both, P(), P()),
        out_specs=(both, wide, wide),
        check_vma=False,
    )
```
